32 devices in a mesh: ctx: 8 (over y, x, core), hd: 4 (over z).
Axes of the slice: x: 2, y: 2, z: 4, core: 2. Of those that a mesh axis runs over, the one named last changes fastest.
Arguments:
- cot: bfloat16 [32, 1024], P('ctx'), may hold values from -768 to 768
- resid: bfloat16 [32, 1024], P('ctx'), may hold values from -17 to 17
- norm_gain: bfloat16 [1024], replicated, may hold values from 0.5 to 1.5
- w_in: bfloat16 [1024, 4096], P(None, 'hd'), may hold values from -0.1875 to 0.1875
- w_out: bfloat16 [4096, 1024], P('hd'), may hold values from -0.09375 to 0.09375
- w_proj: bfloat16 [1024, 1024], P('hd', 'ctx'), may hold values from -0.1875 to 0.1875
- queries: bfloat16 [32, 1024], P('ctx', 'hd'), may hold values from -36 to 36
- keys: bfloat16 [2048, 1024], P('ctx', 'hd'), may hold values from -9 to 9
- values: bfloat16 [2048, 1024], P('ctx', 'hd'), may hold values from -6 to 6
- latent_pos: int32 [32], replicated, may hold values from 1024 to 2047, as said below
- seg_start: int32 [32], replicated, may hold values from 768 to 2046, as said below
Outputs:
- query_grad: bfloat16 [32, 1024], P('ctx', 'hd')
- key_grad: bfloat16 [2048, 1024], P('ctx', 'hd')
- value_grad: bfloat16 [2048, 1024], P('ctx', 'hd')
The draws below stay inside these ranges and needn't reach their ends.
Inputs may be any that keep to these rules, and one draw needn't show every extreme that they name: `latent_pos`: not falling along the latents. seg_start of a latent is 1 to 256 below its latent_pos.
All inputs are finite; a program needn't handle non-finite values.
Results may differ from the reference program's by a relative error of at most 0.012.
Values may be sent and summed in bfloat16 or wider, within the bound.
No kernel may reach another device: no remote copies, remote signals or barrier semaphores. Data moves between devices by JAX's collectives and lax.ppermute only.
A program may use at most 64 MiB of HBM per device.

```python
import math
import jax
import jax.numpy as jnp
from jax import lax

D = 1024
HEADS = 16
FF = 4096
HDIM = 64
CTX_DEV = 256
LATENTS = 32
EVENTS = 2048


def positions(key):
    half = EVENTS // 2
    small_gaps = jax.random.randint(jax.random.fold_in(key, 101), (LATENTS - 1,), 1, 3).astype(jnp.int32)
    jump_count = max(1, LATENTS // 64)
    order = jax.random.permutation(jax.random.fold_in(key, 109), LATENTS - 1).astype(jnp.int32)
    chosen = order[:jump_count]
    weights = jax.random.randint(jax.random.fold_in(key, 110), (jump_count,), 1, 101).astype(jnp.int32)
    remaining = (half - 1 - jnp.sum(small_gaps)).astype(jnp.int32)
    shares = (remaining * weights // jnp.sum(weights)).astype(jnp.int32)
    shares = shares.at[jump_count - 1].add(remaining - jnp.sum(shares)).astype(jnp.int32)
    gaps = small_gaps.at[chosen].add(shares).astype(jnp.int32)
    steps_taken = jnp.concatenate([jnp.zeros((1,), jnp.int32), jnp.cumsum(gaps).astype(jnp.int32)])
    return (half + steps_taken).astype(jnp.int32)


def draw_latent_pos(key, part):
    return positions(key)


def draw_seg_start(key, part):
    spots = positions(key)
    latent_index = jnp.arange(LATENTS, dtype=jnp.int32)
    spans = jax.random.randint(jax.random.fold_in(key, 102), (LATENTS,), 1, CTX_DEV + 1).astype(jnp.int32)
    spans = jnp.where(latent_index == 0, CTX_DEV, jnp.where(latent_index == LATENTS - 1, 1, spans))
    return (spots - spans).astype(jnp.int32)


def draw_queries(key, part):
    base = jax.random.truncated_normal(jax.random.fold_in(key, 105), -4.0, 4.0, (LATENTS, D), jnp.float32)
    return base.astype(jnp.bfloat16)


def draw_keys(key, part):
    base = jax.random.truncated_normal(jax.random.fold_in(key, 106), -4.0, 4.0, (EVENTS, D), jnp.float32)
    return base.astype(jnp.bfloat16)


def draw_resid(key, part):
    base = jax.random.truncated_normal(jax.random.fold_in(key, 107), -4.0, 4.0, (LATENTS, D), jnp.float32)
    return base.astype(jnp.bfloat16)


def levels(stream_key, dims, split, low, largest):
    loudness, own = 1.0, jax.random.fold_in(stream_key, 6)
    for position, shards_of in split:
        heights = jnp.exp(jax.random.uniform(jax.random.fold_in(own, position), (shards_of,), jnp.float32, low / len(split), largest / len(split)))
        loudness = loudness * jnp.repeat(heights, dims[position] // shards_of).reshape([-1 if axis == position else 1 for axis in range(len(dims))])
    return loudness


def bell_draw(own_key, shape, scale, most, shards=(), kind=jnp.bfloat16):
    entries = jax.random.normal(own_key, shape, jnp.float32) * scale
    if len(shards) > 0:
        entries = levels(own_key, shape, shards, -0.22, 0.18) * entries
    return jnp.clip(entries, min=-most, max=most).astype(kind)


def setup_inputs(seed: int = 0) -> dict:
    seeds = jax.random.split(jax.random.key(seed), 12)
    return {
        "cot": bell_draw(seeds[0], (LATENTS, D), 128.0, 768.0, ((0, 8),)),
        "resid": draw_resid(jax.random.fold_in(seeds[11], 71), 0),
        "norm_gain": jnp.clip(1.0 + 0.1 * jax.random.normal(seeds[2], (D,), jnp.float32), 0.5, 1.5).astype(jnp.bfloat16),
        "w_in": bell_draw(seeds[3], (D, FF), D ** -0.5, 0.1875, ((1, 4),)),
        "w_out": bell_draw(seeds[4], (FF, D), FF ** -0.5, 0.09375, ((0, 4),)),
        "w_proj": bell_draw(seeds[5], (D, D), D ** -0.5, 0.1875, ((0, 4), (1, 8))),
        "queries": draw_queries(jax.random.fold_in(seeds[11], 71), 0),
        "keys": draw_keys(jax.random.fold_in(seeds[11], 71), 0),
        "values": bell_draw(seeds[8], (EVENTS, D), 1.0, 6.0, ((0, 8), (1, 4))),
        "latent_pos": draw_latent_pos(jax.random.fold_in(seeds[11], 71), 0),
        "seg_start": draw_seg_start(jax.random.fold_in(seeds[11], 71), 0),
    }


def gelu_slope(values_in):
    inner = 0.7978845608028654 * (values_in + 0.044715 * values_in * values_in * values_in)
    tangent = jnp.tanh(inner)
    return 0.5 * (1.0 + tangent) + 0.5 * values_in * (1.0 - tangent * tangent) * 0.7978845608028654 * (1.0 + 0.134145 * values_in * values_in)

def split_heads(array):
    return array.reshape(array.shape[0], HEADS, HDIM).transpose(1, 0, 2)

def join_heads(array):
    return array.transpose(1, 0, 2).reshape(array.shape[1], HEADS * HDIM)

def reference(cot, resid, norm_gain, w_in, w_out, w_proj, queries, keys, values, latent_pos, seg_start):
    rows_f32 = resid.astype(jnp.float32)
    inv_rms = lax.rsqrt(lax.optimization_barrier(jnp.mean(rows_f32 * rows_f32, axis=-1, keepdims=True)) + 1e-05)
    gain_f32 = norm_gain.astype(jnp.float32)
    normed = (rows_f32 * inv_rms * gain_f32).astype(jnp.bfloat16)
    pre_act = jnp.dot(normed, w_in, preferred_element_type=jnp.float32)
    hidden_grad = jnp.dot(cot, w_out.T, preferred_element_type=jnp.float32)
    pre_grad = (hidden_grad * gelu_slope(pre_act)).astype(jnp.bfloat16)
    normed_grad = jnp.dot(pre_grad, w_in.T, preferred_element_type=jnp.float32)
    weighted = normed_grad * gain_f32
    unit_rows = rows_f32 * inv_rms
    resid_grad = (cot.astype(jnp.float32) + inv_rms * (weighted - unit_rows * lax.optimization_barrier(jnp.mean(weighted * unit_rows, axis=-1, keepdims=True)))).astype(jnp.bfloat16)
    out_grad = jnp.dot(resid_grad, w_proj.T, preferred_element_type=jnp.float32).astype(jnp.bfloat16)
    latents = queries.shape[0]
    events = keys.shape[0]
    event_index = jnp.arange(events, dtype=jnp.int32)
    block_rows = min(latents, 512)
    blocks = latents // block_rows
    factor = 1.0 / math.sqrt(HDIM)

    def one_head(inputs):
        head_q, head_k, head_v, head_do = inputs

        def one_block(carry, block_in):
            key_acc, value_acc = carry
            block_q, block_do, block_pos, block_start = block_in
            scores = factor * jnp.dot(block_q, head_k.T, preferred_element_type=jnp.float32)
            visible = (event_index[None, :] >= block_start[:, None]) & (event_index[None, :] <= block_pos[:, None])
            top = lax.optimization_barrier(jnp.max(jnp.where(visible, scores, -1e+30), axis=1, keepdims=True))
            expo = jnp.where(visible, jnp.exp(scores - top), 0.0)
            probs = expo / lax.optimization_barrier(jnp.sum(expo, axis=1, keepdims=True))
            prob_grad = jnp.dot(block_do, head_v.T, preferred_element_type=jnp.float32)
            delta = lax.optimization_barrier(jnp.sum(probs * prob_grad, axis=1, keepdims=True))
            prob_round = probs.astype(jnp.bfloat16)
            score_grad = (factor * probs * (prob_grad - delta)).astype(jnp.bfloat16)
            value_acc = value_acc + jnp.dot(prob_round.T, block_do, preferred_element_type=jnp.float32)
            key_acc = key_acc + jnp.dot(score_grad.T, block_q, preferred_element_type=jnp.float32)
            query_block = jnp.dot(score_grad, head_k, preferred_element_type=jnp.float32).astype(jnp.bfloat16)
            return ((key_acc, value_acc), query_block)
        block_inputs = (head_q.reshape(blocks, block_rows, HDIM), head_do.reshape(blocks, block_rows, HDIM), latent_pos.reshape(blocks, block_rows), seg_start.reshape(blocks, block_rows))
        start_acc = (jnp.zeros((events, HDIM), jnp.float32), jnp.zeros((events, HDIM), jnp.float32))
        (key_acc, value_acc), query_blocks = lax.scan(one_block, start_acc, block_inputs)
        return (query_blocks.reshape(latents, HDIM), key_acc.astype(jnp.bfloat16), value_acc.astype(jnp.bfloat16))
    query_heads, key_heads, value_heads = lax.map(one_head, (split_heads(queries), split_heads(keys), split_heads(values), split_heads(out_grad)))
    return (join_heads(query_heads), join_heads(key_heads), join_heads(value_heads))
```

```python
import functools
import math

import jax
import jax.numpy as jnp
from jax import lax
from jax.experimental import pallas as pl
from jax.experimental.pallas import tpu as pltpu
from jax.sharding import PartitionSpec as P

HDIM = 64
WINDOW = 256


def joined(value, axis, join):
    pieces = jax.tree.map(lambda part: lax.all_gather(part, axis), value)
    head = jax.tree.map(lambda part: part[0], pieces)
    tail = jax.tree.map(lambda part: part[1:], pieces)
    total, _ = lax.scan(lambda total, slab: (join(total, slab), None), head, tail)
    return total


def gelu_slope(values_in):
    inner = 0.7978845608028654 * (values_in + 0.044715 * values_in * values_in * values_in)
    tangent = jnp.tanh(inner)
    return 0.5 * (1.0 + tangent) + 0.5 * values_in * (
        1.0 - tangent * tangent
    ) * 0.7978845608028654 * (1.0 + 0.134145 * values_in * values_in)


def combine_totals(earlier, later):
    top_first, total_first, weight_first = earlier
    top_second, total_second, weight_second = later
    top_joint = jnp.maximum(top_first, top_second)
    factor_first = jnp.exp(top_first - top_joint)
    factor_second = jnp.exp(top_second - top_joint)
    return (
        top_joint,
        total_first * factor_first + total_second * factor_second,
        weight_first * factor_first + weight_second * factor_second,
    )


def per_device_streamed(
    cot, resid, norm_gain, w_in, w_out, w_proj, queries, keys, values, latent_pos, seg_start
):
    contract_last = (((1,), (1,)), ((), ()))
    rows_f32 = resid.astype(jnp.float32)
    inv_rms = lax.rsqrt(jnp.mean(rows_f32 * rows_f32, axis=-1, keepdims=True) + 1e-05)
    gain_f32 = norm_gain.astype(jnp.float32)
    normed = (rows_f32 * inv_rms * gain_f32).astype(jnp.bfloat16)
    pre_act = jnp.dot(normed, w_in, preferred_element_type=jnp.float32)
    hidden_grad = lax.dot_general(cot, w_out, contract_last, preferred_element_type=jnp.float32)
    pre_grad = (hidden_grad * gelu_slope(pre_act)).astype(jnp.bfloat16)
    partial_grad = lax.dot_general(
        pre_grad, w_in, contract_last, preferred_element_type=jnp.float32
    )
    whole_proj = lax.all_gather(w_proj, "ctx", axis=1, tiled=True)
    normed_grad = lax.psum(partial_grad, "hd")
    weighted = normed_grad * gain_f32
    unit_rows = rows_f32 * inv_rms
    resid_grad = (
        cot.astype(jnp.float32)
        + inv_rms * (weighted - unit_rows * jnp.mean(weighted * unit_rows, axis=-1, keepdims=True))
    ).astype(jnp.bfloat16)
    out_grad = lax.dot_general(
        resid_grad, whole_proj, contract_last, preferred_element_type=jnp.float32
    ).astype(jnp.bfloat16)
    all_queries, all_grads = (
        lax.all_gather(queries, "ctx", axis=0, tiled=True),
        lax.all_gather(out_grad, "ctx", axis=0, tiled=True),
    )
    ctx_count = lax.axis_size("ctx")
    lat_dev = cot.shape[0]
    latents = lat_dev * ctx_count
    blocks = max(1, min(lat_dev, latents // 512))
    per_block = lat_dev // blocks
    block_rows = ctx_count * per_block
    features = queries.shape[1]
    local_heads = features // HDIM
    events_dev = keys.shape[0]
    event_index = lax.axis_index("ctx") * events_dev + jnp.arange(events_dev, dtype=jnp.int32)
    factor = 1.0 / math.sqrt(HDIM)
    head_keys = keys.reshape(events_dev, local_heads, HDIM)
    head_values = values.reshape(events_dev, local_heads, HDIM)

    def block_view(array, which):
        shaped = array.reshape((ctx_count, blocks, per_block) + array.shape[1:])
        picked = lax.dynamic_index_in_dim(shaped, which, 1, keepdims=False)
        return picked.reshape((block_rows,) + array.shape[1:])

    def block_terms(which):
        block_q = block_view(all_queries, which).reshape(block_rows, local_heads, HDIM)
        block_do = block_view(all_grads, which).reshape(block_rows, local_heads, HDIM)
        block_pos = block_view(latent_pos, which)
        block_start = block_view(seg_start, which)
        visible = (event_index[None, :] >= block_start[:, None]) & (
            event_index[None, :] <= block_pos[:, None]
        )
        scores = factor * jnp.einsum(
            "rhe,khe->hrk", block_q, head_keys, preferred_element_type=jnp.float32
        )
        prob_grad = jnp.einsum(
            "rhe,khe->hrk", block_do, head_values, preferred_element_type=jnp.float32
        )
        return (block_q, block_do, visible[None], scores, prob_grad)

    def first_pass(carry, which):
        block_q, block_do, visible, scores, prob_grad = block_terms(which)
        block_top = jnp.max(jnp.where(visible, scores, -1e30), axis=2)
        expo = jnp.where(visible, jnp.exp(scores - block_top[..., None]), 0.0)
        return (carry, (block_top, jnp.sum(expo, axis=2), jnp.sum(expo * prob_grad, axis=2)))

    unused, local_totals = lax.scan(first_pass, jnp.int32(0), jnp.arange(blocks, dtype=jnp.int32))
    tops, totals, weight_sums = joined(local_totals, "ctx", combine_totals)
    deltas = weight_sums / totals

    def second_pass(carry, which):
        key_acc, value_acc = carry
        block_q, block_do, visible, scores, prob_grad = block_terms(which)
        block_top = lax.dynamic_index_in_dim(tops, which, 0, keepdims=False)
        block_total = lax.dynamic_index_in_dim(totals, which, 0, keepdims=False)
        block_delta = lax.dynamic_index_in_dim(deltas, which, 0, keepdims=False)
        expo = jnp.where(visible, jnp.exp(scores - block_top[..., None]), 0.0)
        probs = expo / block_total[..., None]
        prob_round = probs.astype(jnp.bfloat16)
        score_grad = (factor * probs * (prob_grad - block_delta[..., None])).astype(jnp.bfloat16)
        value_acc = value_acc + jnp.einsum(
            "hrk,rhe->khe", prob_round, block_do, preferred_element_type=jnp.float32
        )
        key_acc = key_acc + jnp.einsum(
            "hrk,rhe->khe", score_grad, block_q, preferred_element_type=jnp.float32
        )
        query_part = jnp.einsum(
            "hrk,khe->rhe", score_grad, head_keys, preferred_element_type=jnp.float32
        )
        query_part = query_part.reshape(ctx_count, per_block, features)
        return ((key_acc, value_acc), query_part)

    start_acc = (
        jnp.zeros((events_dev, local_heads, HDIM), jnp.float32),
        jnp.zeros((events_dev, local_heads, HDIM), jnp.float32),
    )
    (key_acc, value_acc), query_parts = lax.scan(
        second_pass, start_acc, jnp.arange(blocks, dtype=jnp.int32)
    )
    query_parts = lax.psum_scatter(query_parts, "ctx", scatter_dimension=1, tiled=True)
    query_grad = query_parts.reshape(lat_dev, features).astype(jnp.bfloat16)
    key_grad = key_acc.reshape(events_dev, features).astype(jnp.bfloat16)
    value_grad = value_acc.reshape(events_dev, features).astype(jnp.bfloat16)
    return (query_grad, key_grad, value_grad)


NT = (((1,), (1,)), ((), ()))
TN = (((0,), (0,)), ((), ()))
Q_ROWS = 16


def pack_kernel(k_ref, v_ref, w_ref, q_ref, out_ref):
    events, half = k_ref.shape[0], w_ref.shape[0] // 2
    out_ref[:events, :] = k_ref[...]
    out_ref[events : 2 * events, :] = v_ref[...]
    base = 2 * events
    out_ref[base : base + half, : w_ref.shape[1]] = w_ref[:half, :]
    out_ref[base : base + half, w_ref.shape[1] :] = w_ref[half:, :]
    rows = q_ref[...].astype(jnp.float32)
    spare = jnp.zeros((Q_ROWS - rows.shape[0], rows.shape[1]), jnp.float32)
    out_ref[base + half :, :] = jnp.concatenate([rows, spare], axis=0).astype(jnp.bfloat16)


def ordered(own, other):
    own, other = own.astype(jnp.float32), other.astype(jnp.float32)
    first = lax.axis_index("ctx") % 2 == 0
    return jnp.where(
        first, jnp.concatenate([own, other], axis=0), jnp.concatenate([other, own], axis=0)
    )


def rms_parts(rows):
    inv_rms = lax.rsqrt(jnp.mean(rows * rows, axis=-1, keepdims=True) + 1e-05)
    return inv_rms, rows * inv_rms


def mlp_kernel(cot_ref, cot_other, resid_ref, resid_other, gain_ref, w_in_ref, w_out_ref, out_ref):
    cot = ordered(cot_ref[...], cot_other[...]).astype(jnp.bfloat16)
    rows = ordered(resid_ref[...], resid_other[...])
    unit = rms_parts(rows)[1]
    normed = (unit * gain_ref[...].astype(jnp.float32)).astype(jnp.bfloat16)
    pre_act = jnp.dot(normed, w_in_ref[...], preferred_element_type=jnp.float32)
    hidden_grad = lax.dot_general(cot, w_out_ref[...], NT, preferred_element_type=jnp.float32)
    pre_grad = (hidden_grad * gelu_slope(pre_act)).astype(jnp.bfloat16)
    out_ref[...] = lax.dot_general(pre_grad, w_in_ref[...], NT, preferred_element_type=jnp.float32)


def resid_kernel(part_ref, arrived_ref, cot_ref, cot_other, resid_ref, resid_other, gain_ref, out_ref):
    rows = ordered(resid_ref[...], resid_other[...])
    inv_rms, unit = rms_parts(rows)
    weighted = (part_ref[...] + arrived_ref[...]) * gain_ref[...].astype(jnp.float32)
    cot = ordered(cot_ref[...], cot_other[...])
    grad = cot + inv_rms * (weighted - unit * jnp.mean(weighted * unit, axis=-1, keepdims=True))
    out_ref[...] = grad.astype(jnp.bfloat16)


def attention_kernel(
    row_offsets, pack_offsets, latents, lat_dev, events_dev, first_block, *refs
):
    n_rows, n_packs = len(row_offsets), len(pack_offsets)
    pos_ref, start_ref = refs[:2]
    row_refs = refs[2 : 2 + n_rows]
    pack_refs = refs[2 + n_rows : 2 + n_rows + n_packs]
    qg_ref, kg_ref, vg_ref, packs, rows_all, qg_all, own_probs, own_scores, sems = refs[
        2 + n_rows + n_packs :
    ]
    me = lax.axis_index("ctx")
    blocks = n_packs
    features = packs.shape[2]
    heads = features // HDIM
    lanes = heads * latents
    factor = 1.0 / math.sqrt(HDIM)
    copies = [
        pltpu.make_async_copy(ref, packs.at[me ^ offset], sems.at[slot])
        for slot, (offset, ref) in enumerate(zip(pack_offsets, pack_refs))
    ]
    for copy in copies:
        copy.start()
    for offset, ref in zip(row_offsets, row_refs):
        rows_all[(me // 2) ^ offset] = ref[...].astype(jnp.float32)
    resid_grad = rows_all[...].reshape(latents, rows_all.shape[2]).astype(jnp.bfloat16)
    for copy in copies:
        copy.wait()

    base = 2 * events_dev
    half = packs.shape[1] - base - Q_ROWS
    halves = [packs[block, base : base + half, :] for block in range(blocks)]
    cols = features // 2
    upper = jnp.concatenate([piece[:, :cols] for piece in halves], axis=1)
    lower = jnp.concatenate([piece[:, cols:] for piece in halves], axis=1)
    out_grad = jnp.concatenate(
        [
            lax.dot_general(resid_grad, piece, NT, preferred_element_type=jnp.float32)
            for piece in (upper, lower)
        ],
        axis=1,
    )
    out_grad = out_grad.astype(jnp.bfloat16).astype(jnp.float32)
    queries = jnp.concatenate(
        [
            packs[block, base + half :, :].astype(jnp.float32)[:lat_dev]
            for block in range(blocks)
        ],
        axis=0,
    )
    lane_head = lax.broadcasted_iota(jnp.int32, (lanes, features), 0) // latents
    own_head = lane_head == lax.broadcasted_iota(jnp.int32, (lanes, features), 1) // HDIM

    def spread(array):
        return jnp.where(own_head, jnp.concatenate([array] * heads, axis=0), 0.0)

    wide_q, wide_g = spread(queries), spread(out_grad)
    wide_qt, wide_gt = wide_q.T.astype(jnp.bfloat16), wide_g.T.astype(jnp.bfloat16)
    wide_q, wide_g = wide_q.astype(jnp.bfloat16), wide_g.astype(jnp.bfloat16)

    lane = lax.broadcasted_iota(jnp.int32, (1, lanes), 1) % latents
    pos, start = jnp.zeros((1, lanes), jnp.int32), jnp.zeros((1, lanes), jnp.int32)
    for latent in range(latents):
        pos = jnp.where(lane == latent, pos_ref[latent], pos)
        start = jnp.where(lane == latent, start_ref[latent], start)

    used = range(first_block, blocks)
    keys = jnp.concatenate([packs[block, :events_dev, :] for block in used], axis=0)
    values = jnp.concatenate([packs[block, events_dev:base, :] for block in used], axis=0)
    spot = first_block * events_dev + lax.broadcasted_iota(jnp.int32, (keys.shape[0], lanes), 0)
    visible = (spot >= start) & (spot <= pos)
    scores = factor * jnp.dot(keys, wide_qt, preferred_element_type=jnp.float32)
    scores = jnp.where(visible, scores, -1e30)
    top = jnp.max(scores, axis=0, keepdims=True)
    expo = jnp.where(visible, jnp.exp(scores - top), 0.0)
    probs = expo * (1.0 / jnp.sum(expo, axis=0, keepdims=True))
    prob_grad = jnp.dot(values, wide_gt, preferred_element_type=jnp.float32)
    delta = jnp.sum(probs * prob_grad, axis=0, keepdims=True)
    score_grad = (factor * probs * (prob_grad - delta)).astype(jnp.bfloat16)
    prob_round = probs.astype(jnp.bfloat16)

    wide = lax.dot_general(score_grad, keys, TN, preferred_element_type=jnp.float32)
    wide = jnp.where(own_head, wide, 0.0)
    total = sum(wide[head * latents : (head + 1) * latents] for head in range(heads))
    qg_all[...] = total.reshape(qg_all.shape)
    pair = qg_all[me // 2]
    mine = jnp.where(me % 2 == 0, pair[:lat_dev], pair[lat_dev:])
    qg_ref[...] = mine.astype(jnp.bfloat16)

    for slot in range(first_block):
        own_probs[slot] = jnp.zeros((events_dev, lanes), jnp.bfloat16)
        own_scores[slot] = jnp.zeros((events_dev, lanes), jnp.bfloat16)
    for slot in used:
        place = (slot - first_block) * events_dev
        own_probs[slot] = prob_round[place : place + events_dev]
        own_scores[slot] = score_grad[place : place + events_dev]
    kg_ref[...] = jnp.dot(own_scores[me], wide_q, preferred_element_type=jnp.float32).astype(
        jnp.bfloat16
    )
    vg_ref[...] = jnp.dot(own_probs[me], wide_g, preferred_element_type=jnp.float32).astype(
        jnp.bfloat16
    )


def swap(array, bit):
    count = lax.axis_size("ctx")
    return lax.ppermute(array, "ctx", [(index, index ^ bit) for index in range(count)])


def swap_hd(array, bit):
    ctx, hd = lax.axis_size("ctx"), lax.axis_size("hd")
    pairs = [
        (c * hd + z, (c ^ 1) * hd + (z ^ bit)) for c in range(ctx) for z in range(hd)
    ]
    return lax.ppermute(array, ("ctx", "hd"), pairs)


def gathered(array, bits):
    pieces = [(0, array)]
    for bit in bits:
        pieces += [(offset ^ bit, swap(piece, bit)) for offset, piece in pieces]
    return pieces


def per_device_packed(
    cot, resid, norm_gain, w_in, w_out, w_proj, queries, keys, values, latent_pos, seg_start
):
    ctx, hd = lax.axis_size("ctx"), lax.axis_size("hd")
    lat_dev, width = cot.shape
    latents = lat_dev * ctx
    events_dev, features = keys.shape
    vmem, anywhere = pl.BlockSpec(memory_space=pltpu.VMEM), pl.BlockSpec(memory_space=pl.ANY)
    smem = pl.BlockSpec(memory_space=pltpu.SMEM)
    gain = norm_gain.reshape(1, width)
    cot_other, resid_other = swap(cot, 1), swap(resid, 1)

    pack_rows = 2 * events_dev + w_proj.shape[0] // 2 + Q_ROWS
    pack = pl.pallas_call(
        pack_kernel,
        out_shape=jax.ShapeDtypeStruct((pack_rows, features), jnp.bfloat16),
        in_specs=[vmem] * 4,
        out_specs=vmem,
        name="pack",
    )(keys, values, w_proj, queries)
    chip_bits = [1 << shift for shift in range(1, ctx.bit_length() - 1)]
    packs = gathered(pack, [bit | 1 for bit in chip_bits])
    packs = packs + [(offset ^ 1, swap(piece, 1)) for offset, piece in packs]

    part = pl.pallas_call(
        mlp_kernel,
        out_shape=jax.ShapeDtypeStruct((2 * lat_dev, width), jnp.float32),
        in_specs=[vmem] * 7,
        out_specs=vmem,
        name="mlp",
    )(cot, cot_other, resid, resid_other, gain, w_in, w_out)
    hd_bits = [1 << shift for shift in range(hd.bit_length() - 1)]
    for bit in hd_bits[:-1]:
        part = part + swap_hd(part, bit)
    arrived = swap_hd(part, hd_bits[-1])
    rows = pl.pallas_call(
        resid_kernel,
        out_shape=jax.ShapeDtypeStruct((2 * lat_dev, width), jnp.bfloat16),
        in_specs=[vmem] * 7,
        out_specs=vmem,
        name="resid",
    )(part, arrived, cot, cot_other, resid, resid_other, gain)
    row_pieces = gathered(rows, [bit | 1 for bit in chip_bits])

    first_event = max(0, events_dev * ctx // 2 - WINDOW)
    lanes = features // HDIM * latents
    kernel = functools.partial(
        attention_kernel,
        [offset >> 1 for offset, _ in row_pieces],
        [offset for offset, _ in packs],
        latents,
        lat_dev,
        events_dev,
        first_event // events_dev,
    )
    return pl.pallas_call(
        kernel,
        out_shape=(
            jax.ShapeDtypeStruct((lat_dev, features), jnp.bfloat16),
            jax.ShapeDtypeStruct((events_dev, features), jnp.bfloat16),
            jax.ShapeDtypeStruct((events_dev, features), jnp.bfloat16),
        ),
        in_specs=[smem] * 2 + [vmem] * len(row_pieces) + [anywhere] * len(packs),
        out_specs=(vmem,) * 3,
        scratch_shapes=[
            pltpu.VMEM((ctx, pack_rows, features), jnp.bfloat16),
            pltpu.VMEM((ctx // 2, 2 * lat_dev, width), jnp.float32),
            pltpu.VMEM((ctx // 2, 2 * lat_dev, features), jnp.float32),
            pltpu.VMEM((ctx, events_dev, lanes), jnp.bfloat16),
            pltpu.VMEM((ctx, events_dev, lanes), jnp.bfloat16),
            pltpu.SemaphoreType.DMA((len(packs),)),
        ],
        compiler_params=pltpu.CompilerParams(vmem_limit_bytes=32 * 1024 * 1024),
        name="attention",
    )(
        latent_pos,
        seg_start,
        *[piece for _, piece in row_pieces],
        *[piece for _, piece in packs],
    )


def solution(mesh):
    in_specs = (
        P("ctx", None),
        P("ctx", None),
        P(),
        P(None, "hd"),
        P("hd", None),
        P("hd", "ctx"),
        P("ctx", "hd"),
        P("ctx", "hd"),
        P("ctx", "hd"),
        P(),
        P(),
    )
    out_specs = (P("ctx", "hd"), P("ctx", "hd"), P("ctx", "hd"))
    ctx, hd = mesh.shape["ctx"], mesh.shape["hd"]

    def per_device(*arrays):
        lat_dev, features = arrays[6].shape
        fits = ctx * arrays[7].size * arrays[7].dtype.itemsize <= 2 * 1024 * 1024
        powers = ctx >= 4 and hd >= 2 and ctx & (ctx - 1) == 0 and hd & (hd - 1) == 0
        aligned = 2 * lat_dev == 8 and features % HDIM == 0 and lat_dev <= Q_ROWS
        if fits and powers and aligned:
            return per_device_packed(*arrays)
        return per_device_streamed(*arrays)

    return jax.shard_map(
        per_device, mesh=mesh, in_specs=in_specs, out_specs=out_specs, check_vma=False
    )
```

```python
import functools
import math

import jax
import jax.numpy as jnp
from jax import lax
from jax.experimental import pallas as pl
from jax.experimental.pallas import tpu as pltpu
from jax.sharding import PartitionSpec as P

HDIM = 64
WINDOW = 256


def joined(value, axis, join):
    pieces = jax.tree.map(lambda part: lax.all_gather(part, axis), value)
    head = jax.tree.map(lambda part: part[0], pieces)
    tail = jax.tree.map(lambda part: part[1:], pieces)
    total, _ = lax.scan(lambda total, slab: (join(total, slab), None), head, tail)
    return total


def gelu_slope(values_in):
    inner = 0.7978845608028654 * (values_in + 0.044715 * values_in * values_in * values_in)
    tangent = jnp.tanh(inner)
    return 0.5 * (1.0 + tangent) + 0.5 * values_in * (
        1.0 - tangent * tangent
    ) * 0.7978845608028654 * (1.0 + 0.134145 * values_in * values_in)


def combine_totals(earlier, later):
    top_first, total_first, weight_first = earlier
    top_second, total_second, weight_second = later
    top_joint = jnp.maximum(top_first, top_second)
    factor_first = jnp.exp(top_first - top_joint)
    factor_second = jnp.exp(top_second - top_joint)
    return (
        top_joint,
        total_first * factor_first + total_second * factor_second,
        weight_first * factor_first + weight_second * factor_second,
    )


def per_device_streamed(
    cot, resid, norm_gain, w_in, w_out, w_proj, queries, keys, values, latent_pos, seg_start
):
    contract_last = (((1,), (1,)), ((), ()))
    rows_f32 = resid.astype(jnp.float32)
    inv_rms = lax.rsqrt(jnp.mean(rows_f32 * rows_f32, axis=-1, keepdims=True) + 1e-05)
    gain_f32 = norm_gain.astype(jnp.float32)
    normed = (rows_f32 * inv_rms * gain_f32).astype(jnp.bfloat16)
    pre_act = jnp.dot(normed, w_in, preferred_element_type=jnp.float32)
    hidden_grad = lax.dot_general(cot, w_out, contract_last, preferred_element_type=jnp.float32)
    pre_grad = (hidden_grad * gelu_slope(pre_act)).astype(jnp.bfloat16)
    partial_grad = lax.dot_general(
        pre_grad, w_in, contract_last, preferred_element_type=jnp.float32
    )
    whole_proj = lax.all_gather(w_proj, "ctx", axis=1, tiled=True)
    normed_grad = lax.psum(partial_grad, "hd")
    weighted = normed_grad * gain_f32
    unit_rows = rows_f32 * inv_rms
    resid_grad = (
        cot.astype(jnp.float32)
        + inv_rms * (weighted - unit_rows * jnp.mean(weighted * unit_rows, axis=-1, keepdims=True))
    ).astype(jnp.bfloat16)
    out_grad = lax.dot_general(
        resid_grad, whole_proj, contract_last, preferred_element_type=jnp.float32
    ).astype(jnp.bfloat16)
    all_queries, all_grads = (
        lax.all_gather(queries, "ctx", axis=0, tiled=True),
        lax.all_gather(out_grad, "ctx", axis=0, tiled=True),
    )
    ctx_count = lax.axis_size("ctx")
    lat_dev = cot.shape[0]
    latents = lat_dev * ctx_count
    blocks = max(1, min(lat_dev, latents // 512))
    per_block = lat_dev // blocks
    block_rows = ctx_count * per_block
    features = queries.shape[1]
    local_heads = features // HDIM
    events_dev = keys.shape[0]
    event_index = lax.axis_index("ctx") * events_dev + jnp.arange(events_dev, dtype=jnp.int32)
    factor = 1.0 / math.sqrt(HDIM)
    head_keys = keys.reshape(events_dev, local_heads, HDIM)
    head_values = values.reshape(events_dev, local_heads, HDIM)

    def block_view(array, which):
        shaped = array.reshape((ctx_count, blocks, per_block) + array.shape[1:])
        picked = lax.dynamic_index_in_dim(shaped, which, 1, keepdims=False)
        return picked.reshape((block_rows,) + array.shape[1:])

    def block_terms(which):
        block_q = block_view(all_queries, which).reshape(block_rows, local_heads, HDIM)
        block_do = block_view(all_grads, which).reshape(block_rows, local_heads, HDIM)
        block_pos = block_view(latent_pos, which)
        block_start = block_view(seg_start, which)
        visible = (event_index[None, :] >= block_start[:, None]) & (
            event_index[None, :] <= block_pos[:, None]
        )
        scores = factor * jnp.einsum(
            "rhe,khe->hrk", block_q, head_keys, preferred_element_type=jnp.float32
        )
        prob_grad = jnp.einsum(
            "rhe,khe->hrk", block_do, head_values, preferred_element_type=jnp.float32
        )
        return (block_q, block_do, visible[None], scores, prob_grad)

    def first_pass(carry, which):
        block_q, block_do, visible, scores, prob_grad = block_terms(which)
        block_top = jnp.max(jnp.where(visible, scores, -1e30), axis=2)
        expo = jnp.where(visible, jnp.exp(scores - block_top[..., None]), 0.0)
        return (carry, (block_top, jnp.sum(expo, axis=2), jnp.sum(expo * prob_grad, axis=2)))

    unused, local_totals = lax.scan(first_pass, jnp.int32(0), jnp.arange(blocks, dtype=jnp.int32))
    tops, totals, weight_sums = joined(local_totals, "ctx", combine_totals)
    deltas = weight_sums / totals

    def second_pass(carry, which):
        key_acc, value_acc = carry
        block_q, block_do, visible, scores, prob_grad = block_terms(which)
        block_top = lax.dynamic_index_in_dim(tops, which, 0, keepdims=False)
        block_total = lax.dynamic_index_in_dim(totals, which, 0, keepdims=False)
        block_delta = lax.dynamic_index_in_dim(deltas, which, 0, keepdims=False)
        expo = jnp.where(visible, jnp.exp(scores - block_top[..., None]), 0.0)
        probs = expo / block_total[..., None]
        prob_round = probs.astype(jnp.bfloat16)
        score_grad = (factor * probs * (prob_grad - block_delta[..., None])).astype(jnp.bfloat16)
        value_acc = value_acc + jnp.einsum(
            "hrk,rhe->khe", prob_round, block_do, preferred_element_type=jnp.float32
        )
        key_acc = key_acc + jnp.einsum(
            "hrk,rhe->khe", score_grad, block_q, preferred_element_type=jnp.float32
        )
        query_part = jnp.einsum(
            "hrk,khe->rhe", score_grad, head_keys, preferred_element_type=jnp.float32
        )
        query_part = query_part.reshape(ctx_count, per_block, features)
        return ((key_acc, value_acc), query_part)

    start_acc = (
        jnp.zeros((events_dev, local_heads, HDIM), jnp.float32),
        jnp.zeros((events_dev, local_heads, HDIM), jnp.float32),
    )
    (key_acc, value_acc), query_parts = lax.scan(
        second_pass, start_acc, jnp.arange(blocks, dtype=jnp.int32)
    )
    query_parts = lax.psum_scatter(query_parts, "ctx", scatter_dimension=1, tiled=True)
    query_grad = query_parts.reshape(lat_dev, features).astype(jnp.bfloat16)
    key_grad = key_acc.reshape(events_dev, features).astype(jnp.bfloat16)
    value_grad = value_acc.reshape(events_dev, features).astype(jnp.bfloat16)
    return (query_grad, key_grad, value_grad)


NT = (((1,), (1,)), ((), ()))
TN = (((0,), (0,)), ((), ()))
Q_ROWS = 16
MLP_PARTS = 4
MLP_AHEAD = 2


def load_kernel(
    k_ref,
    v_ref,
    w_ref,
    q_ref,
    cot_ref,
    resid_ref,
    gain_ref,
    pack_ref,
    rows_ref,
    q_own,
    cot_own,
    resid_own,
    gain_own,
    sems,
):
    events, half, cols = k_ref.shape[0], w_ref.shape[0] // 2, w_ref.shape[1]
    base = 2 * events
    moves = [
        (q_ref, q_own),
        (cot_ref, cot_own),
        (resid_ref, resid_own),
        (gain_ref, gain_own),
        (k_ref, pack_ref.at[pl.ds(0, events)]),
        (v_ref, pack_ref.at[pl.ds(events, events)]),
        (w_ref.at[pl.ds(0, half)], pack_ref.at[pl.ds(base, half), pl.ds(0, cols)]),
        (w_ref.at[pl.ds(half, half)], pack_ref.at[pl.ds(base, half), pl.ds(cols, cols)]),
    ]
    copies = [
        pltpu.make_async_copy(source, target, sems.at[slot])
        for slot, (source, target) in enumerate(moves)
    ]
    for copy in copies:
        copy.start()
    for copy in copies[:4]:
        copy.wait()
    rows = q_own[...].astype(jnp.float32)
    spare = jnp.zeros((Q_ROWS - rows.shape[0], rows.shape[1]), jnp.float32)
    pack_ref[base + half :, :] = jnp.concatenate([rows, spare], axis=0).astype(jnp.bfloat16)
    gain = gain_own[...].astype(jnp.float32).reshape(1, gain_own.shape[0])
    lat_dev = cot_own.shape[0]
    held = [cot_own[...].astype(jnp.float32), resid_own[...].astype(jnp.float32)]
    held += [jnp.broadcast_to(gain, (rows_ref.shape[0] - 2 * lat_dev, gain.shape[1]))]
    rows_ref[...] = jnp.concatenate(held, axis=0).astype(jnp.bfloat16)
    for copy in copies[4:]:
        copy.wait()


def chip_rows(own_ref, other_ref):
    own, other = own_ref[...].astype(jnp.float32), other_ref[...].astype(jnp.float32)
    first = lax.axis_index("ctx") % 2 == 0
    low, high = jnp.where(first, own, other), jnp.where(first, other, own)
    half = own.shape[0] // 4
    cot = jnp.concatenate([low[:half], high[:half]], axis=0)
    rows = jnp.concatenate([low[half : 2 * half], high[half : 2 * half]], axis=0)
    return cot, rows, own[2 * half : 2 * half + 1]


def rms_parts(rows):
    inv_rms = lax.rsqrt(jnp.mean(rows * rows, axis=-1, keepdims=True) + 1e-05)
    return inv_rms, rows * inv_rms


def mlp_kernel(own_ref, other_ref, w_in_ref, w_out_ref, out_ref, w_in, w_out, sems):
    parts, size = w_in.shape[0], w_in.shape[2]
    copies = []
    for part in range(parts):
        span = pl.ds(part * size, size)
        copies.append(
            (
                pltpu.make_async_copy(w_in_ref.at[:, span], w_in.at[part], sems.at[0, part]),
                pltpu.make_async_copy(w_out_ref.at[span], w_out.at[part], sems.at[1, part]),
            )
        )

    def begin(part):
        if part < parts:
            for copy in copies[part]:
                copy.start()

    for part in range(MLP_AHEAD):
        begin(part)
    cot, rows, gain = chip_rows(own_ref, other_ref)
    cot = cot.astype(jnp.bfloat16)
    normed = (rms_parts(rows)[1] * gain).astype(jnp.bfloat16)
    total = jnp.zeros(out_ref.shape, jnp.float32)
    for part in range(parts):
        for copy in copies[part]:
            copy.wait()
        begin(part + MLP_AHEAD)
        up = w_in[part]
        pre_act = jnp.dot(normed, up, preferred_element_type=jnp.float32)
        hidden_grad = lax.dot_general(cot, w_out[part], NT, preferred_element_type=jnp.float32)
        pre_grad = (hidden_grad * gelu_slope(pre_act)).astype(jnp.bfloat16)
        total += lax.dot_general(pre_grad, up, NT, preferred_element_type=jnp.float32)
    out_ref[...] = total


def resid_kernel(part_ref, arrived_ref, own_ref, other_ref, out_ref):
    cot, rows, gain = chip_rows(own_ref, other_ref)
    inv_rms, unit = rms_parts(rows)
    weighted = (part_ref[...] + arrived_ref[...]) * gain
    grad = cot + inv_rms * (weighted - unit * jnp.mean(weighted * unit, axis=-1, keepdims=True))
    out_ref[...] = grad.astype(jnp.bfloat16)


def wide_rows(array, latents):
    features = array.shape[1]
    heads = features // HDIM
    shape = (heads * latents, features)
    row_head = lax.broadcasted_iota(jnp.int32, shape, 0) // latents
    own_head = row_head == lax.broadcasted_iota(jnp.int32, shape, 1) // HDIM
    return jnp.where(own_head, jnp.concatenate([array] * heads, axis=0), 0.0), own_head


def probs_kernel(offsets, latents, lat_dev, events_dev, first_block, *refs):
    pos_ref, start_ref = refs[:2]
    pack_refs = refs[2:-6]
    probs_ref, keys_ref, values_ref, proj_ref, wide_ref, q_all = refs[-6:]
    me = lax.axis_index("ctx")
    even = me % 2 == 0
    base = 2 * events_dev
    pack_rows = base + proj_ref.shape[1] + Q_ROWS
    places = []
    for ref, pair in zip(pack_refs, offsets):
        for slot, offset in enumerate(pair):
            places.append((ref, slot * pack_rows, offset))
    queries = {}
    for ref, row, offset in places:
        block = me ^ jnp.where(even, *offset)
        proj_ref[block] = ref[row + base : row + base + proj_ref.shape[1], :]
        queries[offset] = ref[row + pack_rows - Q_ROWS : row + pack_rows, :].astype(jnp.float32)

        @pl.when(block >= first_block)
        def _(ref=ref, row=row, block=block):
            keys_ref[block - first_block] = ref[row : row + events_dev, :]
            values_ref[block - first_block] = ref[row + events_dev : row + base, :]

    for offset, own in queries.items():
        if offset[0] % 2 == 0:
            other = queries[(offset[0] ^ 1, offset[1] ^ 1)]
            low, high = jnp.where(even, own, other), jnp.where(even, other, own)
            chip = (me ^ jnp.where(even, *offset)) // 2
            q_all[chip] = jnp.concatenate([low[:lat_dev], high[:lat_dev]], axis=0)
    wide_q = wide_rows(q_all[...].reshape(latents, q_all.shape[2]), latents)[0]
    wide_ref[...] = wide_q.astype(jnp.bfloat16)
    wide_qt = wide_q.T.astype(jnp.bfloat16)
    lanes = wide_qt.shape[1]

    lane = lax.broadcasted_iota(jnp.int32, (1, lanes), 1) % latents
    pos, start = jnp.zeros((1, lanes), jnp.int32), jnp.zeros((1, lanes), jnp.int32)
    for latent in range(latents):
        pos = jnp.where(lane == latent, pos_ref[latent], pos)
        start = jnp.where(lane == latent, start_ref[latent], start)
    used, features = keys_ref.shape[0], keys_ref.shape[2]
    keys = keys_ref[...].reshape(used * events_dev, features)
    spot = first_block * events_dev + lax.broadcasted_iota(jnp.int32, (keys.shape[0], lanes), 0)
    visible = (spot >= start) & (spot <= pos)
    scores = (1.0 / math.sqrt(HDIM)) * jnp.dot(keys, wide_qt, preferred_element_type=jnp.float32)
    scores = jnp.where(visible, scores, -1e30)
    top = jnp.max(scores, axis=0, keepdims=True)
    expo = jnp.where(visible, jnp.exp(scores - top), 0.0)
    probs = expo * (1.0 / jnp.sum(expo, axis=0, keepdims=True))
    probs_ref[:first_block] = jnp.zeros((first_block, events_dev, lanes), jnp.float32)
    probs_ref[first_block:] = probs.reshape(used, events_dev, lanes)


def grads_kernel(
    row_offsets,
    latents,
    first_block,
    probs_ref,
    keys_ref,
    values_ref,
    proj_ref,
    wide_ref,
    *refs,
):
    row_refs = refs[: len(row_offsets)]
    qg_ref, kg_ref, vg_ref, rows_all, qg_all, scores_all = refs[len(row_offsets) :]
    me = lax.axis_index("ctx")
    lat_dev = qg_ref.shape[0]
    blocks, events_dev, lanes = probs_ref.shape
    used, features = keys_ref.shape[0], keys_ref.shape[2]
    factor = 1.0 / math.sqrt(HDIM)
    for offset, ref in zip(row_offsets, row_refs):
        rows_all[(me // 2) ^ offset] = ref[...].astype(jnp.float32)
    resid_grad = rows_all[...].reshape(latents, rows_all.shape[2]).astype(jnp.bfloat16)
    cols = features // 2
    upper = jnp.concatenate([proj_ref[block, :, :cols] for block in range(blocks)], axis=1)
    lower = jnp.concatenate([proj_ref[block, :, cols:] for block in range(blocks)], axis=1)
    out_grad = [
        lax.dot_general(resid_grad, piece, NT, preferred_element_type=jnp.float32)
        for piece in (upper, lower)
    ]
    out_grad = jnp.concatenate(out_grad, axis=1).astype(jnp.bfloat16).astype(jnp.float32)
    wide_g, own_head = wide_rows(out_grad, latents)
    wide_gt, wide_g = wide_g.T.astype(jnp.bfloat16), wide_g.astype(jnp.bfloat16)
    keys = keys_ref[...].reshape(used * events_dev, features)
    values = values_ref[...].reshape(used * events_dev, features)
    probs = probs_ref[first_block:].reshape(used * events_dev, lanes)
    prob_grad = jnp.dot(values, wide_gt, preferred_element_type=jnp.float32)
    delta = jnp.sum(probs * prob_grad, axis=0, keepdims=True)
    score_grad = (factor * probs * (prob_grad - delta)).astype(jnp.bfloat16)
    scores_all[:first_block] = jnp.zeros((first_block, events_dev, lanes), jnp.bfloat16)
    scores_all[first_block:] = score_grad.reshape(used, events_dev, lanes)

    wide = lax.dot_general(score_grad, keys, TN, preferred_element_type=jnp.float32)
    wide = jnp.where(own_head, wide, 0.0)
    total = sum(wide[head * latents : (head + 1) * latents] for head in range(lanes // latents))
    qg_all[...] = total.reshape(qg_all.shape)
    pair = qg_all[me // 2]
    mine = jnp.where(me % 2 == 0, pair[:lat_dev], pair[lat_dev:])
    qg_ref[...] = mine.astype(jnp.bfloat16)
    prob_round = probs_ref[me].astype(jnp.bfloat16)
    vg_ref[...] = jnp.dot(prob_round, wide_g, preferred_element_type=jnp.float32).astype(
        jnp.bfloat16
    )
    kg_ref[...] = jnp.dot(scores_all[me], wide_ref[...], preferred_element_type=jnp.float32).astype(
        jnp.bfloat16
    )


def swap(array, bit, odd_bit=None):
    bits = (bit, bit if odd_bit is None else odd_bit)
    count = lax.axis_size("ctx")
    return lax.ppermute(array, "ctx", [(index, index ^ bits[index % 2]) for index in range(count)])


def swap_hd(array, bit):
    ctx, hd = lax.axis_size("ctx"), lax.axis_size("hd")
    pairs = [
        (c * hd + z, (c ^ 1) * hd + (z ^ bit)) for c in range(ctx) for z in range(hd)
    ]
    return lax.ppermute(array, ("ctx", "hd"), pairs)


def after(array, *others):
    return lax.optimization_barrier((array, *others))[0]


def in_hbm(array):
    return pltpu.with_memory_space_constraint(array, pltpu.HBM)


def params(mebibytes):
    return pltpu.CompilerParams(vmem_limit_bytes=mebibytes * 1024 * 1024)


def per_device_packed(
    cot, resid, norm_gain, w_in, w_out, w_proj, queries, keys, values, latent_pos, seg_start
):
    ctx, hd = lax.axis_size("ctx"), lax.axis_size("hd")
    lat_dev, width = cot.shape
    latents = lat_dev * ctx
    events_dev, features = keys.shape
    hidden = w_in.shape[1]
    vmem = pl.BlockSpec(memory_space=pltpu.VMEM)
    smem = pl.BlockSpec(memory_space=pltpu.SMEM)
    hbm = pl.BlockSpec(memory_space=pltpu.HBM)
    pack_rows = 2 * events_dev + w_proj.shape[0] // 2 + Q_ROWS
    pack, own_rows = pl.pallas_call(
        load_kernel,
        out_shape=(
            jax.ShapeDtypeStruct((pack_rows, features), jnp.bfloat16),
            jax.ShapeDtypeStruct((4 * lat_dev, width), jnp.bfloat16),
        ),
        in_specs=[hbm] * 7,
        out_specs=(vmem,) * 2,
        scratch_shapes=[
            pltpu.VMEM((lat_dev, features), jnp.bfloat16),
            pltpu.VMEM((lat_dev, width), jnp.bfloat16),
            pltpu.VMEM((lat_dev, width), jnp.bfloat16),
            pltpu.VMEM((width,), jnp.bfloat16),
            pltpu.SemaphoreType.DMA((8,)),
        ],
        compiler_params=params(8),
        name="load",
    )(*[in_hbm(array) for array in (keys, values, w_proj, queries, cot, resid, norm_gain)])
    other_rows = swap(own_rows, 1)

    chip_bits = [1 << shift for shift in range(1, ctx.bit_length() - 1)]
    hd_bits = [1 << shift for shift in range(hd.bit_length() - 1)]
    steps = (tuple(chip_bits), tuple(reversed(chip_bits)))
    first_piece = swap(pack, *steps[0])
    part = pl.pallas_call(
        mlp_kernel,
        out_shape=jax.ShapeDtypeStruct((2 * lat_dev, width), jnp.float32),
        in_specs=[vmem] * 2 + [hbm] * 2,
        out_specs=vmem,
        scratch_shapes=[
            pltpu.VMEM((MLP_PARTS, width, hidden // MLP_PARTS), jnp.bfloat16),
            pltpu.VMEM((MLP_PARTS, hidden // MLP_PARTS, width), jnp.bfloat16),
            pltpu.SemaphoreType.DMA((2, MLP_PARTS)),
        ],
        compiler_params=params(16),
        cost_estimate=pl.CostEstimate(
            flops=12 * lat_dev * w_in.size, bytes_accessed=4 * w_in.size, transcendentals=0
        ),
        name="mlp",
    )(own_rows, other_rows, in_hbm(w_in), in_hbm(w_out))
    first_pair = jnp.concatenate([pack, after(first_piece, part)], axis=0)
    second_pair = swap(first_pair, *steps[1])
    for bit in hd_bits[:-1]:
        part = part + swap_hd(part, bit)
    first_other = swap(after(first_pair, part), 1)
    arrived = swap_hd(part, hd_bits[-1])
    rows = pl.pallas_call(
        resid_kernel,
        out_shape=jax.ShapeDtypeStruct((2 * lat_dev, width), jnp.bfloat16),
        in_specs=[vmem] * 4,
        out_specs=vmem,
        compiler_params=params(8),
        name="resid",
    )(part, arrived, own_rows, other_rows)
    row_x, row_y = (swap(rows, bit | 1) for bit in chip_bits)
    row_xy = swap(after(row_x, second_pair), chip_bits[1] | 1)
    second_other = swap(after(second_pair, row_x), 1)

    corner = tuple(step ^ other for step, other in zip(*steps))
    turn = lambda pair: (pair[1] ^ 1, pair[0] ^ 1)
    near, far = [(0, 0), steps[0]], [steps[1], corner]
    offsets = [near, [turn(pair) for pair in near], far, [turn(pair) for pair in far]]
    first_block = max(0, events_dev * ctx // 2 - WINDOW) // events_dev
    lanes = features // HDIM * latents
    probs, used_keys, used_values, proj, wide_q = pl.pallas_call(
        functools.partial(probs_kernel, offsets, latents, lat_dev, events_dev, first_block),
        out_shape=(
            jax.ShapeDtypeStruct((ctx, events_dev, lanes), jnp.float32),
            jax.ShapeDtypeStruct((ctx - first_block, events_dev, features), jnp.bfloat16),
            jax.ShapeDtypeStruct((ctx - first_block, events_dev, features), jnp.bfloat16),
            jax.ShapeDtypeStruct((ctx, w_proj.shape[0] // 2, features), jnp.bfloat16),
            jax.ShapeDtypeStruct((lanes, features), jnp.bfloat16),
        ),
        in_specs=[smem] * 2 + [vmem] * 4,
        out_specs=(vmem,) * 5,
        scratch_shapes=[pltpu.VMEM((ctx // 2, 2 * lat_dev, features), jnp.float32)],
        compiler_params=params(24),
        cost_estimate=pl.CostEstimate(
            flops=2 * ctx * keys.size * lanes, bytes_accessed=8 * keys.size, transcendentals=0
        ),
        name="probs",
    )(latent_pos, seg_start, first_pair, first_other, second_pair, second_other)
    return pl.pallas_call(
        functools.partial(
            grads_kernel, [0, *[bit // 2 for bit in chip_bits], sum(chip_bits) // 2], latents, first_block
        ),
        out_shape=(
            jax.ShapeDtypeStruct((lat_dev, features), jnp.bfloat16),
            jax.ShapeDtypeStruct((events_dev, features), jnp.bfloat16),
            jax.ShapeDtypeStruct((events_dev, features), jnp.bfloat16),
        ),
        in_specs=[vmem] * 9,
        out_specs=(vmem,) * 3,
        scratch_shapes=[
            pltpu.VMEM((ctx // 2, 2 * lat_dev, width), jnp.float32),
            pltpu.VMEM((ctx // 2, 2 * lat_dev, features), jnp.float32),
            pltpu.VMEM((ctx, events_dev, lanes), jnp.bfloat16),
        ],
        compiler_params=params(24),
        name="grads",
    )(probs, used_keys, used_values, proj, wide_q, rows, row_x, row_y, row_xy)


def solution(mesh):
    in_specs = (
        P("ctx", None),
        P("ctx", None),
        P(),
        P(None, "hd"),
        P("hd", None),
        P("hd", "ctx"),
        P("ctx", "hd"),
        P("ctx", "hd"),
        P("ctx", "hd"),
        P(),
        P(),
    )
    out_specs = (P("ctx", "hd"), P("ctx", "hd"), P("ctx", "hd"))
    ctx, hd = mesh.shape["ctx"], mesh.shape["hd"]

    def per_device(*arrays):
        lat_dev, features = arrays[6].shape
        fits = ctx * arrays[7].size * arrays[7].dtype.itemsize <= 2 * 1024 * 1024
        powers = ctx == 8 and hd >= 2 and ctx & (ctx - 1) == 0 and hd & (hd - 1) == 0
        aligned = 2 * lat_dev == 8 and features % HDIM == 0 and lat_dev <= Q_ROWS
        if fits and powers and aligned:
            return per_device_packed(*arrays)
        return per_device_streamed(*arrays)

    return jax.shard_map(
        per_device, mesh=mesh, in_specs=in_specs, out_specs=out_specs, check_vma=False
    )
```

```python
import functools
import math

import jax
import jax.numpy as jnp
from jax import lax
from jax.experimental import pallas as pl
from jax.experimental.pallas import tpu as pltpu
from jax.sharding import PartitionSpec as P

HDIM = 64
WINDOW = 256


def joined(value, axis, join):
    pieces = jax.tree.map(lambda part: lax.all_gather(part, axis), value)
    head = jax.tree.map(lambda part: part[0], pieces)
    tail = jax.tree.map(lambda part: part[1:], pieces)
    total, _ = lax.scan(lambda total, slab: (join(total, slab), None), head, tail)
    return total


def gelu_slope(values_in):
    inner = 0.7978845608028654 * (values_in + 0.044715 * values_in * values_in * values_in)
    tangent = jnp.tanh(inner)
    return 0.5 * (1.0 + tangent) + 0.5 * values_in * (
        1.0 - tangent * tangent
    ) * 0.7978845608028654 * (1.0 + 0.134145 * values_in * values_in)


def combine_totals(earlier, later):
    top_first, total_first, weight_first = earlier
    top_second, total_second, weight_second = later
    top_joint = jnp.maximum(top_first, top_second)
    factor_first = jnp.exp(top_first - top_joint)
    factor_second = jnp.exp(top_second - top_joint)
    return (
        top_joint,
        total_first * factor_first + total_second * factor_second,
        weight_first * factor_first + weight_second * factor_second,
    )


def per_device_streamed(
    cot, resid, norm_gain, w_in, w_out, w_proj, queries, keys, values, latent_pos, seg_start
):
    contract_last = (((1,), (1,)), ((), ()))
    rows_f32 = resid.astype(jnp.float32)
    inv_rms = lax.rsqrt(jnp.mean(rows_f32 * rows_f32, axis=-1, keepdims=True) + 1e-05)
    gain_f32 = norm_gain.astype(jnp.float32)
    normed = (rows_f32 * inv_rms * gain_f32).astype(jnp.bfloat16)
    pre_act = jnp.dot(normed, w_in, preferred_element_type=jnp.float32)
    hidden_grad = lax.dot_general(cot, w_out, contract_last, preferred_element_type=jnp.float32)
    pre_grad = (hidden_grad * gelu_slope(pre_act)).astype(jnp.bfloat16)
    partial_grad = lax.dot_general(
        pre_grad, w_in, contract_last, preferred_element_type=jnp.float32
    )
    whole_proj = lax.all_gather(w_proj, "ctx", axis=1, tiled=True)
    normed_grad = lax.psum(partial_grad, "hd")
    weighted = normed_grad * gain_f32
    unit_rows = rows_f32 * inv_rms
    resid_grad = (
        cot.astype(jnp.float32)
        + inv_rms * (weighted - unit_rows * jnp.mean(weighted * unit_rows, axis=-1, keepdims=True))
    ).astype(jnp.bfloat16)
    out_grad = lax.dot_general(
        resid_grad, whole_proj, contract_last, preferred_element_type=jnp.float32
    ).astype(jnp.bfloat16)
    all_queries, all_grads = (
        lax.all_gather(queries, "ctx", axis=0, tiled=True),
        lax.all_gather(out_grad, "ctx", axis=0, tiled=True),
    )
    ctx_count = lax.axis_size("ctx")
    lat_dev = cot.shape[0]
    latents = lat_dev * ctx_count
    blocks = max(1, min(lat_dev, latents // 512))
    per_block = lat_dev // blocks
    block_rows = ctx_count * per_block
    features = queries.shape[1]
    local_heads = features // HDIM
    events_dev = keys.shape[0]
    event_index = lax.axis_index("ctx") * events_dev + jnp.arange(events_dev, dtype=jnp.int32)
    factor = 1.0 / math.sqrt(HDIM)
    head_keys = keys.reshape(events_dev, local_heads, HDIM)
    head_values = values.reshape(events_dev, local_heads, HDIM)

    def block_view(array, which):
        shaped = array.reshape((ctx_count, blocks, per_block) + array.shape[1:])
        picked = lax.dynamic_index_in_dim(shaped, which, 1, keepdims=False)
        return picked.reshape((block_rows,) + array.shape[1:])

    def block_terms(which):
        block_q = block_view(all_queries, which).reshape(block_rows, local_heads, HDIM)
        block_do = block_view(all_grads, which).reshape(block_rows, local_heads, HDIM)
        block_pos = block_view(latent_pos, which)
        block_start = block_view(seg_start, which)
        visible = (event_index[None, :] >= block_start[:, None]) & (
            event_index[None, :] <= block_pos[:, None]
        )
        scores = factor * jnp.einsum(
            "rhe,khe->hrk", block_q, head_keys, preferred_element_type=jnp.float32
        )
        prob_grad = jnp.einsum(
            "rhe,khe->hrk", block_do, head_values, preferred_element_type=jnp.float32
        )
        return (block_q, block_do, visible[None], scores, prob_grad)

    def first_pass(carry, which):
        block_q, block_do, visible, scores, prob_grad = block_terms(which)
        block_top = jnp.max(jnp.where(visible, scores, -1e30), axis=2)
        expo = jnp.where(visible, jnp.exp(scores - block_top[..., None]), 0.0)
        return (carry, (block_top, jnp.sum(expo, axis=2), jnp.sum(expo * prob_grad, axis=2)))

    unused, local_totals = lax.scan(first_pass, jnp.int32(0), jnp.arange(blocks, dtype=jnp.int32))
    tops, totals, weight_sums = joined(local_totals, "ctx", combine_totals)
    deltas = weight_sums / totals

    def second_pass(carry, which):
        key_acc, value_acc = carry
        block_q, block_do, visible, scores, prob_grad = block_terms(which)
        block_top = lax.dynamic_index_in_dim(tops, which, 0, keepdims=False)
        block_total = lax.dynamic_index_in_dim(totals, which, 0, keepdims=False)
        block_delta = lax.dynamic_index_in_dim(deltas, which, 0, keepdims=False)
        expo = jnp.where(visible, jnp.exp(scores - block_top[..., None]), 0.0)
        probs = expo / block_total[..., None]
        prob_round = probs.astype(jnp.bfloat16)
        score_grad = (factor * probs * (prob_grad - block_delta[..., None])).astype(jnp.bfloat16)
        value_acc = value_acc + jnp.einsum(
            "hrk,rhe->khe", prob_round, block_do, preferred_element_type=jnp.float32
        )
        key_acc = key_acc + jnp.einsum(
            "hrk,rhe->khe", score_grad, block_q, preferred_element_type=jnp.float32
        )
        query_part = jnp.einsum(
            "hrk,khe->rhe", score_grad, head_keys, preferred_element_type=jnp.float32
        )
        query_part = query_part.reshape(ctx_count, per_block, features)
        return ((key_acc, value_acc), query_part)

    start_acc = (
        jnp.zeros((events_dev, local_heads, HDIM), jnp.float32),
        jnp.zeros((events_dev, local_heads, HDIM), jnp.float32),
    )
    (key_acc, value_acc), query_parts = lax.scan(
        second_pass, start_acc, jnp.arange(blocks, dtype=jnp.int32)
    )
    query_parts = lax.psum_scatter(query_parts, "ctx", scatter_dimension=1, tiled=True)
    query_grad = query_parts.reshape(lat_dev, features).astype(jnp.bfloat16)
    key_grad = key_acc.reshape(events_dev, features).astype(jnp.bfloat16)
    value_grad = value_acc.reshape(events_dev, features).astype(jnp.bfloat16)
    return (query_grad, key_grad, value_grad)


NT = (((1,), (1,)), ((), ()))
TN = (((0,), (0,)), ((), ()))
Q_ROWS = 16
LATE_ROWS = 96
MLP_PARTS = 2


def load_kernel(
    k_ref,
    v_ref,
    w_ref,
    q_ref,
    cot_ref,
    resid_ref,
    gain_ref,
    pack_ref,
    rows_ref,
    q_own,
    cot_own,
    resid_own,
    gain_own,
    sems,
):
    events, half, cols = k_ref.shape[0], w_ref.shape[0] // 2, w_ref.shape[1]
    base = 2 * events
    moves = [
        (q_ref, q_own),
        (cot_ref, cot_own),
        (resid_ref, resid_own),
        (gain_ref, gain_own),
        (k_ref, pack_ref.at[pl.ds(0, events)]),
        (v_ref, pack_ref.at[pl.ds(events, events)]),
        (w_ref.at[pl.ds(0, half)], pack_ref.at[pl.ds(base, half), pl.ds(0, cols)]),
        (w_ref.at[pl.ds(half, half)], pack_ref.at[pl.ds(base, half), pl.ds(cols, cols)]),
    ]
    copies = [
        pltpu.make_async_copy(source, target, sems.at[slot])
        for slot, (source, target) in enumerate(moves)
    ]
    for copy in copies:
        copy.start()
    for copy in copies[:4]:
        copy.wait()
    rows = q_own[...].astype(jnp.float32)
    spare = jnp.zeros((Q_ROWS - rows.shape[0], rows.shape[1]), jnp.float32)
    pack_ref[base + half :, :] = jnp.concatenate([rows, spare], axis=0).astype(jnp.bfloat16)
    gain = gain_own[...].astype(jnp.float32).reshape(1, gain_own.shape[0])
    lat_dev = cot_own.shape[0]
    held = [cot_own[...].astype(jnp.float32), resid_own[...].astype(jnp.float32)]
    held += [jnp.broadcast_to(gain, (rows_ref.shape[0] - 2 * lat_dev, gain.shape[1]))]
    rows_ref[...] = jnp.concatenate(held, axis=0).astype(jnp.bfloat16)
    for copy in copies[4:]:
        copy.wait()


def chip_rows(own_ref, other_ref):
    own, other = own_ref[...].astype(jnp.float32), other_ref[...].astype(jnp.float32)
    first = lax.axis_index("ctx") % 2 == 0
    low, high = jnp.where(first, own, other), jnp.where(first, other, own)
    half = own.shape[0] // 4
    cot = jnp.concatenate([low[:half], high[:half]], axis=0)
    rows = jnp.concatenate([low[half : 2 * half], high[half : 2 * half]], axis=0)
    return cot, rows, own[2 * half : 2 * half + 1]


def rms_parts(rows):
    inv_rms = lax.rsqrt(jnp.mean(rows * rows, axis=-1, keepdims=True) + 1e-05)
    return inv_rms, rows * inv_rms


def mlp_kernel(own_ref, other_ref, w_in_ref, w_out_ref, out_ref, w_in, sems):
    parts, size = w_in.shape[0], w_in.shape[2]
    copies = []
    for part in range(parts):
        span = pl.ds(part * size, size)
        copies.append(pltpu.make_async_copy(w_in_ref.at[:, span], w_in.at[part], sems.at[part]))
    for copy in copies:
        copy.start()
    cot, rows, gain = chip_rows(own_ref, other_ref)
    normed = (rms_parts(rows)[1] * gain).astype(jnp.bfloat16)
    hidden_grad = lax.dot_general(
        cot.astype(jnp.bfloat16), w_out_ref[...], NT, preferred_element_type=jnp.float32
    )
    total = jnp.zeros(out_ref.shape, jnp.float32)
    for part, copy in enumerate(copies):
        copy.wait()
        up = w_in[part]
        pre_act = jnp.dot(normed, up, preferred_element_type=jnp.float32)
        span = slice(part * size, (part + 1) * size)
        pre_grad = (hidden_grad[:, span] * gelu_slope(pre_act)).astype(jnp.bfloat16)
        total += lax.dot_general(pre_grad, up, NT, preferred_element_type=jnp.float32)
    out_ref[...] = total


def resid_kernel(part_ref, arrived_ref, own_ref, other_ref, out_ref):
    cot, rows, gain = chip_rows(own_ref, other_ref)
    inv_rms, unit = rms_parts(rows)
    weighted = (part_ref[...] + arrived_ref[...]) * gain
    grad = cot + inv_rms * (weighted - unit * jnp.mean(weighted * unit, axis=-1, keepdims=True))
    out_ref[...] = grad.astype(jnp.bfloat16)


def wide_rows(array, latents):
    features = array.shape[1]
    heads = features // HDIM
    shape = (heads * latents, features)
    row_head = lax.broadcasted_iota(jnp.int32, shape, 0) // latents
    own_head = row_head == lax.broadcasted_iota(jnp.int32, shape, 1) // HDIM
    return jnp.where(own_head, jnp.concatenate([array] * heads, axis=0), 0.0), own_head


def straight(index):
    return (index ^ (index >> 1) ^ (index >> 2)) % 2 == 0


def probs_kernel(offsets, latents, lat_dev, events_dev, first_block, *refs):
    pos_ref, start_ref = refs[:2]
    pack_refs = refs[2:-6]
    probs_ref, keys_ref, values_ref, proj_ref, wide_ref, q_all = refs[-6:]
    me = lax.axis_index("ctx")
    even = me % 2 == 0
    base = 2 * events_dev
    pack_rows = base + proj_ref.shape[1] + Q_ROWS
    places = []
    for ref, pair in zip(pack_refs, offsets):
        for slot, offset in enumerate(pair):
            places.append((ref, slot * pack_rows, offset))
    queries = {}
    for ref, row, offset in places:
        block = me ^ jnp.where(straight(me), *offset)
        proj_ref[block] = ref[row + base : row + base + proj_ref.shape[1], :]
        queries[offset] = ref[row + pack_rows - Q_ROWS : row + pack_rows, :].astype(jnp.float32)

        @pl.when(block >= first_block)
        def _(ref=ref, row=row, block=block):
            keys_ref[block - first_block] = ref[row : row + events_dev, :]
            values_ref[block - first_block] = ref[row + events_dev : row + base, :]

    for offset, own in queries.items():
        if offset[0] % 2 == 0:
            other = queries[(offset[0] ^ 1, offset[1] ^ 1)]
            low, high = jnp.where(even, own, other), jnp.where(even, other, own)
            chip = (me ^ jnp.where(straight(me), *offset)) // 2
            q_all[chip] = jnp.concatenate([low[:lat_dev], high[:lat_dev]], axis=0)
    wide_q = wide_rows(q_all[...].reshape(latents, q_all.shape[2]), latents)[0]
    wide_ref[...] = wide_q.astype(jnp.bfloat16)
    wide_qt = wide_q.T.astype(jnp.bfloat16)
    lanes = wide_qt.shape[1]

    lane = lax.broadcasted_iota(jnp.int32, (1, lanes), 1) % latents
    pos, start = jnp.zeros((1, lanes), jnp.int32), jnp.zeros((1, lanes), jnp.int32)
    for latent in range(latents):
        pos = jnp.where(lane == latent, pos_ref[latent], pos)
        start = jnp.where(lane == latent, start_ref[latent], start)
    used, features = keys_ref.shape[0], keys_ref.shape[2]
    keys = keys_ref[...].reshape(used * events_dev, features)
    spot = first_block * events_dev + lax.broadcasted_iota(jnp.int32, (keys.shape[0], lanes), 0)
    visible = (spot >= start) & (spot <= pos)
    scores = (1.0 / math.sqrt(HDIM)) * jnp.dot(keys, wide_qt, preferred_element_type=jnp.float32)
    scores = jnp.where(visible, scores, -1e30)
    top = jnp.max(scores, axis=0, keepdims=True)
    expo = jnp.where(visible, jnp.exp(scores - top), 0.0)
    probs = expo * (1.0 / jnp.sum(expo, axis=0, keepdims=True))
    probs_ref[:first_block] = jnp.zeros((first_block, events_dev, lanes), jnp.float32)
    probs_ref[first_block:] = probs.reshape(used, events_dev, lanes)


def grads_kernel(
    row_offsets,
    pair_offset,
    latents,
    first_block,
    probs_ref,
    keys_ref,
    values_ref,
    proj_ref,
    wide_ref,
    *refs,
):
    row_refs = refs[: len(row_offsets)]
    qg_ref, kg_ref, vg_ref, rows_all, qg_all, scores_all = refs[len(row_offsets) :]
    me = lax.axis_index("ctx")
    lat_dev = qg_ref.shape[0]
    blocks, events_dev, lanes = probs_ref.shape
    used, features = keys_ref.shape[0], keys_ref.shape[2]
    factor = 1.0 / math.sqrt(HDIM)
    for offset, ref in zip(row_offsets, row_refs):
        pair = ref[...].astype(jnp.float32)
        rows_all[(me // 2) ^ offset] = pair[: 2 * lat_dev]
        rows_all[(me // 2) ^ offset ^ pair_offset] = pair[2 * lat_dev :]
    resid_grad = rows_all[...].reshape(latents, rows_all.shape[2]).astype(jnp.bfloat16)
    cols = features // 2
    upper = jnp.concatenate([proj_ref[block, :, :cols] for block in range(blocks)], axis=1)
    lower = jnp.concatenate([proj_ref[block, :, cols:] for block in range(blocks)], axis=1)
    out_grad = [
        lax.dot_general(resid_grad, piece, NT, preferred_element_type=jnp.float32)
        for piece in (upper, lower)
    ]
    out_grad = jnp.concatenate(out_grad, axis=1).astype(jnp.bfloat16).astype(jnp.float32)
    wide_g, own_head = wide_rows(out_grad, latents)
    wide_gt, wide_g = wide_g.T.astype(jnp.bfloat16), wide_g.astype(jnp.bfloat16)
    keys = keys_ref[...].reshape(used * events_dev, features)
    values = values_ref[...].reshape(used * events_dev, features)
    probs = probs_ref[first_block:].reshape(used * events_dev, lanes)
    prob_grad = jnp.dot(values, wide_gt, preferred_element_type=jnp.float32)
    delta = jnp.sum(probs * prob_grad, axis=0, keepdims=True)
    score_grad = (factor * probs * (prob_grad - delta)).astype(jnp.bfloat16)
    scores_all[:first_block] = jnp.zeros((first_block, events_dev, lanes), jnp.bfloat16)
    scores_all[first_block:] = score_grad.reshape(used, events_dev, lanes)

    wide = lax.dot_general(score_grad, keys, TN, preferred_element_type=jnp.float32)
    wide = jnp.where(own_head, wide, 0.0)
    total = sum(wide[head * latents : (head + 1) * latents] for head in range(lanes // latents))
    qg_all[...] = total.reshape(qg_all.shape)
    pair = qg_all[me // 2]
    mine = jnp.where(me % 2 == 0, pair[:lat_dev], pair[lat_dev:])
    qg_ref[...] = mine.astype(jnp.bfloat16)
    prob_round = probs_ref[me].astype(jnp.bfloat16)
    vg_ref[...] = jnp.dot(prob_round, wide_g, preferred_element_type=jnp.float32).astype(
        jnp.bfloat16
    )
    kg_ref[...] = jnp.dot(scores_all[me], wide_ref[...], preferred_element_type=jnp.float32).astype(
        jnp.bfloat16
    )


def swap(array, bit, other_bit=None):
    bits = (bit, bit if other_bit is None else other_bit)
    pairs = [(c, c ^ bits[c.bit_count() % 2]) for c in range(lax.axis_size("ctx"))]
    return lax.ppermute(array, "ctx", pairs)


def swap_hd(array, bit):
    ctx, hd = lax.axis_size("ctx"), lax.axis_size("hd")
    pairs = [
        (c * hd + z, (c ^ 1) * hd + (z ^ bit)) for c in range(ctx) for z in range(hd)
    ]
    return lax.ppermute(array, ("ctx", "hd"), pairs)


def after(array, *others):
    return lax.optimization_barrier((array, *others))[0]


def in_hbm(array):
    return pltpu.with_memory_space_constraint(array, pltpu.HBM)


def params(mebibytes):
    return pltpu.CompilerParams(vmem_limit_bytes=mebibytes * 1024 * 1024)


def per_device_packed(
    cot, resid, norm_gain, w_in, w_out, w_proj, queries, keys, values, latent_pos, seg_start
):
    ctx, hd = lax.axis_size("ctx"), lax.axis_size("hd")
    lat_dev, width = cot.shape
    latents = lat_dev * ctx
    events_dev, features = keys.shape
    hidden = w_in.shape[1]
    vmem = pl.BlockSpec(memory_space=pltpu.VMEM)
    smem = pl.BlockSpec(memory_space=pltpu.SMEM)
    hbm = pl.BlockSpec(memory_space=pltpu.HBM)
    pack_rows = 2 * events_dev + w_proj.shape[0] // 2 + Q_ROWS
    pack, own_rows = pl.pallas_call(
        load_kernel,
        out_shape=(
            jax.ShapeDtypeStruct((pack_rows, features), jnp.bfloat16),
            jax.ShapeDtypeStruct((4 * lat_dev, width), jnp.bfloat16),
        ),
        in_specs=[hbm] * 7,
        out_specs=(vmem,) * 2,
        scratch_shapes=[
            pltpu.VMEM((lat_dev, features), jnp.bfloat16),
            pltpu.VMEM((lat_dev, width), jnp.bfloat16),
            pltpu.VMEM((lat_dev, width), jnp.bfloat16),
            pltpu.VMEM((width,), jnp.bfloat16),
            pltpu.SemaphoreType.DMA((8,)),
        ],
        compiler_params=params(8),
        name="load",
    )(*[in_hbm(array) for array in (keys, values, w_proj, queries, cot, resid, norm_gain)])
    other_rows = swap(own_rows, 1)
    near_out = swap(w_out, 1)

    chip_bits = [1 << shift for shift in range(1, ctx.bit_length() - 1)]
    hd_bits = [1 << shift for shift in range(hd.bit_length() - 1)]
    steps = (tuple(bit | 1 for bit in chip_bits), tuple(bit | 1 for bit in reversed(chip_bits)))
    first_piece = swap(pack, *steps[0])
    part = pl.pallas_call(
        mlp_kernel,
        out_shape=jax.ShapeDtypeStruct((2 * lat_dev, width), jnp.float32),
        in_specs=[vmem] * 2 + [hbm, vmem],
        out_specs=vmem,
        scratch_shapes=[
            pltpu.VMEM((MLP_PARTS, width, hidden // MLP_PARTS), jnp.bfloat16),
            pltpu.SemaphoreType.DMA((MLP_PARTS,)),
        ],
        compiler_params=params(16),
        cost_estimate=pl.CostEstimate(
            flops=12 * lat_dev * w_in.size, bytes_accessed=4 * w_in.size, transcendentals=0
        ),
        name="mlp",
    )(own_rows, other_rows, in_hbm(w_in), near_out)
    first_pair = jnp.concatenate([pack, after(first_piece, part)], axis=0)
    second_pair = swap(first_pair, *steps[1])
    for bit in hd_bits[:-1]:
        part = part + swap_hd(part, bit)
    early_rows = first_pair.shape[0] - LATE_ROWS
    early_other = swap(after(first_pair, part)[:early_rows], 1)
    late_other = swap(after(first_pair, part)[early_rows:], 1)
    first_other = jnp.concatenate([early_other, late_other], axis=0)
    arrived = swap_hd(part, hd_bits[-1])
    arrived = after(arrived, early_other)
    rows = pl.pallas_call(
        resid_kernel,
        out_shape=jax.ShapeDtypeStruct((2 * lat_dev, width), jnp.bfloat16),
        in_specs=[vmem] * 4,
        out_specs=vmem,
        compiler_params=params(8),
        name="resid",
    )(part, arrived, own_rows, other_rows)
    rows = after(rows, late_other)
    row_x = swap(rows, chip_bits[0] | 1)
    row_pair = jnp.concatenate([rows, row_x], axis=0)
    row_far = swap(row_pair, chip_bits[1] | 1)
    second_other = swap(after(second_pair, row_x), 1)

    corner = tuple(step ^ other for step, other in zip(*steps))
    turn = lambda pair: (pair[1] ^ 1, pair[0] ^ 1)
    near, far = [(0, 0), steps[0]], [steps[1], corner]
    offsets = [near, [turn(pair) for pair in near], far, [turn(pair) for pair in far]]
    first_block = max(0, events_dev * ctx // 2 - WINDOW) // events_dev
    lanes = features // HDIM * latents
    probs, used_keys, used_values, proj, wide_q = pl.pallas_call(
        functools.partial(probs_kernel, offsets, latents, lat_dev, events_dev, first_block),
        out_shape=(
            jax.ShapeDtypeStruct((ctx, events_dev, lanes), jnp.float32),
            jax.ShapeDtypeStruct((ctx - first_block, events_dev, features), jnp.bfloat16),
            jax.ShapeDtypeStruct((ctx - first_block, events_dev, features), jnp.bfloat16),
            jax.ShapeDtypeStruct((ctx, w_proj.shape[0] // 2, features), jnp.bfloat16),
            jax.ShapeDtypeStruct((lanes, features), jnp.bfloat16),
        ),
        in_specs=[smem] * 2 + [vmem] * 4,
        out_specs=(vmem,) * 5,
        scratch_shapes=[pltpu.VMEM((ctx // 2, 2 * lat_dev, features), jnp.float32)],
        compiler_params=params(24),
        cost_estimate=pl.CostEstimate(
            flops=2 * ctx * keys.size * lanes, bytes_accessed=8 * keys.size, transcendentals=0
        ),
        name="probs",
    )(latent_pos, seg_start, first_pair, first_other, second_pair, second_other)
    return pl.pallas_call(
        functools.partial(
            grads_kernel, [0, chip_bits[1] // 2], chip_bits[0] // 2, latents, first_block
        ),
        out_shape=(
            jax.ShapeDtypeStruct((lat_dev, features), jnp.bfloat16),
            jax.ShapeDtypeStruct((events_dev, features), jnp.bfloat16),
            jax.ShapeDtypeStruct((events_dev, features), jnp.bfloat16),
        ),
        in_specs=[vmem] * 7,
        out_specs=(vmem,) * 3,
        scratch_shapes=[
            pltpu.VMEM((ctx // 2, 2 * lat_dev, width), jnp.float32),
            pltpu.VMEM((ctx // 2, 2 * lat_dev, features), jnp.float32),
            pltpu.VMEM((ctx, events_dev, lanes), jnp.bfloat16),
        ],
        compiler_params=params(24),
        name="grads",
    )(probs, used_keys, used_values, proj, wide_q, row_pair, row_far)


def solution(mesh):
    in_specs = (
        P("ctx", None),
        P("ctx", None),
        P(),
        P(None, "hd"),
        P("hd", None),
        P("hd", "ctx"),
        P("ctx", "hd"),
        P("ctx", "hd"),
        P("ctx", "hd"),
        P(),
        P(),
    )
    out_specs = (P("ctx", "hd"), P("ctx", "hd"), P("ctx", "hd"))
    ctx, hd = mesh.shape["ctx"], mesh.shape["hd"]

    def per_device(*arrays):
        lat_dev, features = arrays[6].shape
        fits = ctx * arrays[7].size * arrays[7].dtype.itemsize <= 2 * 1024 * 1024
        powers = ctx == 8 and hd >= 2 and ctx & (ctx - 1) == 0 and hd & (hd - 1) == 0
        aligned = 2 * lat_dev == 8 and features % HDIM == 0 and lat_dev <= Q_ROWS
        if fits and powers and aligned:
            return per_device_packed(*arrays)
        return per_device_streamed(*arrays)

    return jax.shard_map(
        per_device, mesh=mesh, in_specs=in_specs, out_specs=out_specs, check_vma=False
    )
```

```python
import functools
import math

import jax
import jax.numpy as jnp
from jax import lax
from jax.experimental import pallas as pl
from jax.experimental.pallas import tpu as pltpu
from jax.sharding import PartitionSpec as P

HDIM = 64
WINDOW = 256


def joined(value, axis, join):
    pieces = jax.tree.map(lambda part: lax.all_gather(part, axis), value)
    head = jax.tree.map(lambda part: part[0], pieces)
    tail = jax.tree.map(lambda part: part[1:], pieces)
    total, _ = lax.scan(lambda total, slab: (join(total, slab), None), head, tail)
    return total


def gelu_slope(values_in):
    inner = 0.7978845608028654 * (values_in + 0.044715 * values_in * values_in * values_in)
    tangent = jnp.tanh(inner)
    return 0.5 * (1.0 + tangent) + 0.5 * values_in * (
        1.0 - tangent * tangent
    ) * 0.7978845608028654 * (1.0 + 0.134145 * values_in * values_in)


def combine_totals(earlier, later):
    top_first, total_first, weight_first = earlier
    top_second, total_second, weight_second = later
    top_joint = jnp.maximum(top_first, top_second)
    factor_first = jnp.exp(top_first - top_joint)
    factor_second = jnp.exp(top_second - top_joint)
    return (
        top_joint,
        total_first * factor_first + total_second * factor_second,
        weight_first * factor_first + weight_second * factor_second,
    )


def per_device_streamed(
    cot, resid, norm_gain, w_in, w_out, w_proj, queries, keys, values, latent_pos, seg_start
):
    contract_last = (((1,), (1,)), ((), ()))
    rows_f32 = resid.astype(jnp.float32)
    inv_rms = lax.rsqrt(jnp.mean(rows_f32 * rows_f32, axis=-1, keepdims=True) + 1e-05)
    gain_f32 = norm_gain.astype(jnp.float32)
    normed = (rows_f32 * inv_rms * gain_f32).astype(jnp.bfloat16)
    pre_act = jnp.dot(normed, w_in, preferred_element_type=jnp.float32)
    hidden_grad = lax.dot_general(cot, w_out, contract_last, preferred_element_type=jnp.float32)
    pre_grad = (hidden_grad * gelu_slope(pre_act)).astype(jnp.bfloat16)
    partial_grad = lax.dot_general(
        pre_grad, w_in, contract_last, preferred_element_type=jnp.float32
    )
    whole_proj = lax.all_gather(w_proj, "ctx", axis=1, tiled=True)
    normed_grad = lax.psum(partial_grad, "hd")
    weighted = normed_grad * gain_f32
    unit_rows = rows_f32 * inv_rms
    resid_grad = (
        cot.astype(jnp.float32)
        + inv_rms * (weighted - unit_rows * jnp.mean(weighted * unit_rows, axis=-1, keepdims=True))
    ).astype(jnp.bfloat16)
    out_grad = lax.dot_general(
        resid_grad, whole_proj, contract_last, preferred_element_type=jnp.float32
    ).astype(jnp.bfloat16)
    all_queries, all_grads = (
        lax.all_gather(queries, "ctx", axis=0, tiled=True),
        lax.all_gather(out_grad, "ctx", axis=0, tiled=True),
    )
    ctx_count = lax.axis_size("ctx")
    lat_dev = cot.shape[0]
    latents = lat_dev * ctx_count
    blocks = max(1, min(lat_dev, latents // 512))
    per_block = lat_dev // blocks
    block_rows = ctx_count * per_block
    features = queries.shape[1]
    local_heads = features // HDIM
    events_dev = keys.shape[0]
    event_index = lax.axis_index("ctx") * events_dev + jnp.arange(events_dev, dtype=jnp.int32)
    factor = 1.0 / math.sqrt(HDIM)
    head_keys = keys.reshape(events_dev, local_heads, HDIM)
    head_values = values.reshape(events_dev, local_heads, HDIM)

    def block_view(array, which):
        shaped = array.reshape((ctx_count, blocks, per_block) + array.shape[1:])
        picked = lax.dynamic_index_in_dim(shaped, which, 1, keepdims=False)
        return picked.reshape((block_rows,) + array.shape[1:])

    def block_terms(which):
        block_q = block_view(all_queries, which).reshape(block_rows, local_heads, HDIM)
        block_do = block_view(all_grads, which).reshape(block_rows, local_heads, HDIM)
        block_pos = block_view(latent_pos, which)
        block_start = block_view(seg_start, which)
        visible = (event_index[None, :] >= block_start[:, None]) & (
            event_index[None, :] <= block_pos[:, None]
        )
        scores = factor * jnp.einsum(
            "rhe,khe->hrk", block_q, head_keys, preferred_element_type=jnp.float32
        )
        prob_grad = jnp.einsum(
            "rhe,khe->hrk", block_do, head_values, preferred_element_type=jnp.float32
        )
        return (block_q, block_do, visible[None], scores, prob_grad)

    def first_pass(carry, which):
        block_q, block_do, visible, scores, prob_grad = block_terms(which)
        block_top = jnp.max(jnp.where(visible, scores, -1e30), axis=2)
        expo = jnp.where(visible, jnp.exp(scores - block_top[..., None]), 0.0)
        return (carry, (block_top, jnp.sum(expo, axis=2), jnp.sum(expo * prob_grad, axis=2)))

    unused, local_totals = lax.scan(first_pass, jnp.int32(0), jnp.arange(blocks, dtype=jnp.int32))
    tops, totals, weight_sums = joined(local_totals, "ctx", combine_totals)
    deltas = weight_sums / totals

    def second_pass(carry, which):
        key_acc, value_acc = carry
        block_q, block_do, visible, scores, prob_grad = block_terms(which)
        block_top = lax.dynamic_index_in_dim(tops, which, 0, keepdims=False)
        block_total = lax.dynamic_index_in_dim(totals, which, 0, keepdims=False)
        block_delta = lax.dynamic_index_in_dim(deltas, which, 0, keepdims=False)
        expo = jnp.where(visible, jnp.exp(scores - block_top[..., None]), 0.0)
        probs = expo / block_total[..., None]
        prob_round = probs.astype(jnp.bfloat16)
        score_grad = (factor * probs * (prob_grad - block_delta[..., None])).astype(jnp.bfloat16)
        value_acc = value_acc + jnp.einsum(
            "hrk,rhe->khe", prob_round, block_do, preferred_element_type=jnp.float32
        )
        key_acc = key_acc + jnp.einsum(
            "hrk,rhe->khe", score_grad, block_q, preferred_element_type=jnp.float32
        )
        query_part = jnp.einsum(
            "hrk,khe->rhe", score_grad, head_keys, preferred_element_type=jnp.float32
        )
        query_part = query_part.reshape(ctx_count, per_block, features)
        return ((key_acc, value_acc), query_part)

    start_acc = (
        jnp.zeros((events_dev, local_heads, HDIM), jnp.float32),
        jnp.zeros((events_dev, local_heads, HDIM), jnp.float32),
    )
    (key_acc, value_acc), query_parts = lax.scan(
        second_pass, start_acc, jnp.arange(blocks, dtype=jnp.int32)
    )
    query_parts = lax.psum_scatter(query_parts, "ctx", scatter_dimension=1, tiled=True)
    query_grad = query_parts.reshape(lat_dev, features).astype(jnp.bfloat16)
    key_grad = key_acc.reshape(events_dev, features).astype(jnp.bfloat16)
    value_grad = value_acc.reshape(events_dev, features).astype(jnp.bfloat16)
    return (query_grad, key_grad, value_grad)


NT = (((1,), (1,)), ((), ()))
TN = (((0,), (0,)), ((), ()))
Q_ROWS = 16
LATE_ROWS = 96
MLP_PARTS = 2


def load_kernel(
    k_ref,
    v_ref,
    w_ref,
    q_ref,
    cot_ref,
    resid_ref,
    gain_ref,
    pos_ref,
    start_ref,
    pack_ref,
    rows_ref,
    marks_ref,
    q_own,
    cot_own,
    resid_own,
    gain_own,
    pos_own,
    start_own,
    sems,
):
    events, half, cols = k_ref.shape[0], w_ref.shape[0] // 2, w_ref.shape[1]
    base = 2 * events
    moves = [
        (q_ref, q_own),
        (cot_ref, cot_own),
        (resid_ref, resid_own),
        (gain_ref, gain_own),
        (pos_ref, pos_own),
        (start_ref, start_own),
        (k_ref, pack_ref.at[pl.ds(0, events)]),
        (v_ref, pack_ref.at[pl.ds(events, events)]),
        (w_ref.at[pl.ds(0, half)], pack_ref.at[pl.ds(base, half), pl.ds(0, cols)]),
        (w_ref.at[pl.ds(half, half)], pack_ref.at[pl.ds(base, half), pl.ds(cols, cols)]),
    ]
    copies = [
        pltpu.make_async_copy(source, target, sems.at[slot])
        for slot, (source, target) in enumerate(moves)
    ]
    for copy in copies:
        copy.start()
    for copy in copies[:6]:
        copy.wait()
    rows = q_own[...].astype(jnp.float32)
    spare = jnp.zeros((Q_ROWS - rows.shape[0], rows.shape[1]), jnp.float32)
    pack_ref[base + half :, :] = jnp.concatenate([rows, spare], axis=0).astype(jnp.bfloat16)
    gain = gain_own[...].astype(jnp.float32).reshape(1, gain_own.shape[0])
    lat_dev = cot_own.shape[0]
    held = [cot_own[...].astype(jnp.float32), resid_own[...].astype(jnp.float32)]
    held += [jnp.broadcast_to(gain, (rows_ref.shape[0] - 2 * lat_dev, gain.shape[1]))]
    rows_ref[...] = jnp.concatenate(held, axis=0).astype(jnp.bfloat16)
    latents = pos_ref.shape[0]
    lane = lax.broadcasted_iota(jnp.int32, marks_ref.shape, 1) % latents
    first = lax.broadcasted_iota(jnp.int32, marks_ref.shape, 0) == 0
    marks = jnp.zeros(marks_ref.shape, jnp.int32)
    for latent in range(latents):
        pair = jnp.where(first, pos_own[latent], start_own[latent])
        marks = jnp.where(lane == latent, pair, marks)
    marks_ref[...] = marks
    for copy in copies[6:]:
        copy.wait()


def chip_rows(own_ref, other_ref):
    own, other = own_ref[...].astype(jnp.float32), other_ref[...].astype(jnp.float32)
    first = lax.axis_index("ctx") % 2 == 0
    low, high = jnp.where(first, own, other), jnp.where(first, other, own)
    half = own.shape[0] // 4
    cot = jnp.concatenate([low[:half], high[:half]], axis=0)
    rows = jnp.concatenate([low[half : 2 * half], high[half : 2 * half]], axis=0)
    return cot, rows, own[2 * half : 2 * half + 1]


def rms_parts(rows):
    inv_rms = lax.rsqrt(jnp.mean(rows * rows, axis=-1, keepdims=True) + 1e-05)
    return inv_rms, rows * inv_rms


def mlp_kernel(own_ref, other_ref, w_in_ref, w_out_ref, out_ref, w_in, sems):
    parts, size = w_in.shape[0], w_in.shape[2]
    copies = []
    for part in range(parts):
        span = pl.ds(part * size, size)
        copies.append(pltpu.make_async_copy(w_in_ref.at[:, span], w_in.at[part], sems.at[part]))
    for copy in copies:
        copy.start()
    cot, rows, gain = chip_rows(own_ref, other_ref)
    normed = (rms_parts(rows)[1] * gain).astype(jnp.bfloat16)
    hidden_grad = lax.dot_general(
        cot.astype(jnp.bfloat16), w_out_ref[...], NT, preferred_element_type=jnp.float32
    )
    total = jnp.zeros(out_ref.shape, jnp.float32)
    for part, copy in enumerate(copies):
        copy.wait()
        up = w_in[part]
        pre_act = jnp.dot(normed, up, preferred_element_type=jnp.float32)
        span = slice(part * size, (part + 1) * size)
        pre_grad = (hidden_grad[:, span] * gelu_slope(pre_act)).astype(jnp.bfloat16)
        total += lax.dot_general(pre_grad, up, NT, preferred_element_type=jnp.float32)
    out_ref[...] = total


def resid_kernel(part_ref, arrived_ref, own_ref, other_ref, out_ref):
    cot, rows, gain = chip_rows(own_ref, other_ref)
    inv_rms, unit = rms_parts(rows)
    weighted = (part_ref[...] + arrived_ref[...]) * gain
    grad = cot + inv_rms * (weighted - unit * jnp.mean(weighted * unit, axis=-1, keepdims=True))
    out_ref[...] = grad.astype(jnp.bfloat16)


def wide_rows(array, latents):
    features = array.shape[1]
    heads = features // HDIM
    shape = (heads * latents, features)
    row_head = lax.broadcasted_iota(jnp.int32, shape, 0) // latents
    own_head = row_head == lax.broadcasted_iota(jnp.int32, shape, 1) // HDIM
    return jnp.where(own_head, jnp.concatenate([array] * heads, axis=0), 0.0), own_head


def straight(index):
    return (index ^ (index >> 1) ^ (index >> 2)) % 2 == 0


def probs_kernel(offsets, latents, lat_dev, events_dev, first_block, *refs):
    marks_ref = refs[0]
    pack_refs = refs[1:-6]
    probs_ref, keys_ref, values_ref, proj_ref, wide_ref, q_all = refs[-6:]
    me = lax.axis_index("ctx")
    even = me % 2 == 0
    base = 2 * events_dev
    pack_rows = base + proj_ref.shape[1] + Q_ROWS
    places = []
    for ref, pair in zip(pack_refs, offsets):
        for slot, offset in enumerate(pair):
            places.append((ref, slot * pack_rows, offset))
    queries = {}
    for ref, row, offset in places:
        block = me ^ jnp.where(straight(me), *offset)
        proj_ref[block] = ref[row + base : row + base + proj_ref.shape[1], :]
        queries[offset] = ref[row + pack_rows - Q_ROWS : row + pack_rows, :].astype(jnp.float32)

        @pl.when(block >= first_block)
        def _(ref=ref, row=row, block=block):
            keys_ref[block - first_block] = ref[row : row + events_dev, :]
            values_ref[block - first_block] = ref[row + events_dev : row + base, :]

    for offset, own in queries.items():
        if offset[0] % 2 == 0:
            other = queries[(offset[0] ^ 1, offset[1] ^ 1)]
            low, high = jnp.where(even, own, other), jnp.where(even, other, own)
            chip = (me ^ jnp.where(straight(me), *offset)) // 2
            q_all[chip] = jnp.concatenate([low[:lat_dev], high[:lat_dev]], axis=0)
    wide_q = wide_rows(q_all[...].reshape(latents, q_all.shape[2]), latents)[0]
    wide_q = wide_q * (1.0 / math.sqrt(HDIM))
    wide_ref[...] = wide_q.astype(jnp.bfloat16)
    wide_qt = wide_q.T.astype(jnp.bfloat16)
    lanes = wide_qt.shape[1]

    pos, start = marks_ref[0:1, :], marks_ref[1:2, :]
    used, features = keys_ref.shape[0], keys_ref.shape[2]
    top = jnp.full((1, lanes), -1e30, jnp.float32)
    for slot in range(used):
        scores = jnp.dot(keys_ref[slot], wide_qt, preferred_element_type=jnp.float32)
        spot = (first_block + slot) * events_dev + lax.broadcasted_iota(jnp.int32, scores.shape, 0)
        scores = jnp.where((spot >= start) & (spot <= pos), scores, -1e30)
        probs_ref[first_block + slot] = scores
        top = jnp.maximum(top, jnp.max(scores, axis=0, keepdims=True))
    total = jnp.zeros((1, lanes), jnp.float32)
    for slot in range(used):
        expo = jnp.exp(probs_ref[first_block + slot] - top)
        probs_ref[first_block + slot] = expo
        total += jnp.sum(expo, axis=0, keepdims=True)
    share = 1.0 / total
    for slot in range(used):
        probs_ref[first_block + slot] = probs_ref[first_block + slot] * share
    probs_ref[:first_block] = jnp.zeros((first_block, events_dev, lanes), jnp.float32)


def grads_kernel(
    row_offsets,
    pair_offset,
    latents,
    first_block,
    probs_ref,
    keys_ref,
    values_ref,
    proj_ref,
    wide_ref,
    *refs,
):
    row_refs = refs[: len(row_offsets)]
    qg_ref, kg_ref, vg_ref, rows_all, qg_all, grad_all, scores_all = refs[len(row_offsets) :]
    me = lax.axis_index("ctx")
    lat_dev = qg_ref.shape[0]
    blocks, events_dev, lanes = probs_ref.shape
    used, features = keys_ref.shape[0], keys_ref.shape[2]
    factor = 1.0 / math.sqrt(HDIM)
    for offset, ref in zip(row_offsets, row_refs):
        pair = ref[...].astype(jnp.float32)
        rows_all[(me // 2) ^ offset] = pair[: 2 * lat_dev]
        rows_all[(me // 2) ^ offset ^ pair_offset] = pair[2 * lat_dev :]
    resid_grad = rows_all[...].reshape(latents, rows_all.shape[2]).astype(jnp.bfloat16)
    cols = features // 2
    upper = jnp.concatenate([proj_ref[block, :, :cols] for block in range(blocks)], axis=1)
    lower = jnp.concatenate([proj_ref[block, :, cols:] for block in range(blocks)], axis=1)
    out_grad = [
        lax.dot_general(resid_grad, piece, NT, preferred_element_type=jnp.float32)
        for piece in (upper, lower)
    ]
    out_grad = jnp.concatenate(out_grad, axis=1).astype(jnp.bfloat16).astype(jnp.float32)
    wide_g, own_head = wide_rows(out_grad, latents)
    wide_gt, wide_g = wide_g.T.astype(jnp.bfloat16), wide_g.astype(jnp.bfloat16)
    delta = jnp.zeros((1, lanes), jnp.float32)
    for slot in range(used):
        prob_grad = jnp.dot(values_ref[slot], wide_gt, preferred_element_type=jnp.float32)
        grad_all[slot] = prob_grad
        delta += jnp.sum(probs_ref[first_block + slot] * prob_grad, axis=0, keepdims=True)
    wide = jnp.zeros((lanes, features), jnp.float32)
    for slot in range(used):
        score_grad = probs_ref[first_block + slot] * (grad_all[slot] - delta)
        score_grad = score_grad.astype(jnp.bfloat16)
        scores_all[first_block + slot] = score_grad
        wide += lax.dot_general(
            score_grad, keys_ref[slot], TN, preferred_element_type=jnp.float32
        )
    for slot in range(first_block):
        scores_all[slot] = jnp.zeros((events_dev, lanes), jnp.bfloat16)
    wide = jnp.where(own_head, wide, 0.0)
    total = sum(wide[head * latents : (head + 1) * latents] for head in range(lanes // latents))
    qg_all[...] = total.reshape(qg_all.shape)
    pair = qg_all[me // 2]
    mine = jnp.where(me % 2 == 0, pair[:lat_dev], pair[lat_dev:])
    qg_ref[...] = (factor * mine).astype(jnp.bfloat16)
    prob_round = probs_ref[me].astype(jnp.bfloat16)
    vg_ref[...] = jnp.dot(prob_round, wide_g, preferred_element_type=jnp.float32).astype(
        jnp.bfloat16
    )
    kg_ref[...] = jnp.dot(scores_all[me], wide_ref[...], preferred_element_type=jnp.float32).astype(
        jnp.bfloat16
    )


def swap(array, bit, other_bit=None):
    bits = (bit, bit if other_bit is None else other_bit)
    pairs = [(c, c ^ bits[c.bit_count() % 2]) for c in range(lax.axis_size("ctx"))]
    return lax.ppermute(array, "ctx", pairs)


def swap_hd(array, bit):
    ctx, hd = lax.axis_size("ctx"), lax.axis_size("hd")
    pairs = [
        (c * hd + z, (c ^ 1) * hd + (z ^ bit)) for c in range(ctx) for z in range(hd)
    ]
    return lax.ppermute(array, ("ctx", "hd"), pairs)


def after(array, *others):
    return lax.optimization_barrier((array, *others))[0]


def in_hbm(array):
    return pltpu.with_memory_space_constraint(array, pltpu.HBM)


def params(mebibytes):
    return pltpu.CompilerParams(vmem_limit_bytes=mebibytes * 1024 * 1024)


def per_device_packed(
    cot, resid, norm_gain, w_in, w_out, w_proj, queries, keys, values, latent_pos, seg_start
):
    ctx, hd = lax.axis_size("ctx"), lax.axis_size("hd")
    lat_dev, width = cot.shape
    latents = lat_dev * ctx
    events_dev, features = keys.shape
    hidden = w_in.shape[1]
    vmem = pl.BlockSpec(memory_space=pltpu.VMEM)
    hbm = pl.BlockSpec(memory_space=pltpu.HBM)
    pack_rows = 2 * events_dev + w_proj.shape[0] // 2 + Q_ROWS
    lanes = features // HDIM * latents
    pack, own_rows, marks = pl.pallas_call(
        load_kernel,
        out_shape=(
            jax.ShapeDtypeStruct((pack_rows, features), jnp.bfloat16),
            jax.ShapeDtypeStruct((4 * lat_dev, width), jnp.bfloat16),
            jax.ShapeDtypeStruct((8, lanes), jnp.int32),
        ),
        in_specs=[hbm] * 9,
        out_specs=(vmem,) * 3,
        scratch_shapes=[
            pltpu.VMEM((lat_dev, features), jnp.bfloat16),
            pltpu.VMEM((lat_dev, width), jnp.bfloat16),
            pltpu.VMEM((lat_dev, width), jnp.bfloat16),
            pltpu.VMEM((width,), jnp.bfloat16),
            pltpu.SMEM((latents,), jnp.int32),
            pltpu.SMEM((latents,), jnp.int32),
            pltpu.SemaphoreType.DMA((10,)),
        ],
        compiler_params=params(8),
        name="load",
    )(
        *[
            in_hbm(array)
            for array in (
                keys, values, w_proj, queries, cot, resid, norm_gain, latent_pos, seg_start
            )
        ]
    )
    other_rows = swap(own_rows, 1)
    near_out = swap(w_out, 1)

    chip_bits = [1 << shift for shift in range(1, ctx.bit_length() - 1)]
    hd_bits = [1 << shift for shift in range(hd.bit_length() - 1)]
    steps = (tuple(bit | 1 for bit in chip_bits), tuple(bit | 1 for bit in reversed(chip_bits)))
    first_piece = swap(pack, *steps[0])
    part = pl.pallas_call(
        mlp_kernel,
        out_shape=jax.ShapeDtypeStruct((2 * lat_dev, width), jnp.float32),
        in_specs=[vmem] * 2 + [hbm, vmem],
        out_specs=vmem,
        scratch_shapes=[
            pltpu.VMEM((MLP_PARTS, width, hidden // MLP_PARTS), jnp.bfloat16),
            pltpu.SemaphoreType.DMA((MLP_PARTS,)),
        ],
        compiler_params=params(16),
        cost_estimate=pl.CostEstimate(
            flops=12 * lat_dev * w_in.size, bytes_accessed=4 * w_in.size, transcendentals=0
        ),
        name="mlp",
    )(own_rows, other_rows, in_hbm(w_in), near_out)
    first_pair = jnp.concatenate([pack, after(first_piece, part)], axis=0)
    second_pair = swap(first_pair, *steps[1])
    for bit in hd_bits[:-1]:
        part = part + swap_hd(part, bit)
    early_rows = first_pair.shape[0] - LATE_ROWS
    early_other = swap(after(first_pair, part)[:early_rows], 1)
    late_other = swap(after(first_pair, part)[early_rows:], 1)
    first_other = jnp.concatenate([early_other, late_other], axis=0)
    arrived = swap_hd(part, hd_bits[-1])
    arrived = after(arrived, early_other)
    rows = pl.pallas_call(
        resid_kernel,
        out_shape=jax.ShapeDtypeStruct((2 * lat_dev, width), jnp.bfloat16),
        in_specs=[vmem] * 4,
        out_specs=vmem,
        compiler_params=params(8),
        name="resid",
    )(part, arrived, own_rows, other_rows)
    rows = after(rows, late_other)
    row_x = swap(rows, chip_bits[0] | 1)
    row_pair = jnp.concatenate([rows, row_x], axis=0)
    row_far = swap(row_pair, chip_bits[1] | 1)
    second_other = swap(after(second_pair, row_x), 1)

    corner = tuple(step ^ other for step, other in zip(*steps))
    turn = lambda pair: (pair[1] ^ 1, pair[0] ^ 1)
    near, far = [(0, 0), steps[0]], [steps[1], corner]
    offsets = [near, [turn(pair) for pair in near], far, [turn(pair) for pair in far]]
    first_block = max(0, events_dev * ctx // 2 - WINDOW) // events_dev
    lanes = features // HDIM * latents
    probs, used_keys, used_values, proj, wide_q = pl.pallas_call(
        functools.partial(probs_kernel, offsets, latents, lat_dev, events_dev, first_block),
        out_shape=(
            jax.ShapeDtypeStruct((ctx, events_dev, lanes), jnp.float32),
            jax.ShapeDtypeStruct((ctx - first_block, events_dev, features), jnp.bfloat16),
            jax.ShapeDtypeStruct((ctx - first_block, events_dev, features), jnp.bfloat16),
            jax.ShapeDtypeStruct((ctx, w_proj.shape[0] // 2, features), jnp.bfloat16),
            jax.ShapeDtypeStruct((lanes, features), jnp.bfloat16),
        ),
        in_specs=[vmem] * 5,
        out_specs=(vmem,) * 5,
        scratch_shapes=[pltpu.VMEM((ctx // 2, 2 * lat_dev, features), jnp.float32)],
        compiler_params=params(24),
        cost_estimate=pl.CostEstimate(
            flops=2 * ctx * keys.size * lanes, bytes_accessed=8 * keys.size, transcendentals=0
        ),
        name="probs",
    )(marks, first_pair, first_other, second_pair, second_other)
    return pl.pallas_call(
        functools.partial(
            grads_kernel, [0, chip_bits[1] // 2], chip_bits[0] // 2, latents, first_block
        ),
        out_shape=(
            jax.ShapeDtypeStruct((lat_dev, features), jnp.bfloat16),
            jax.ShapeDtypeStruct((events_dev, features), jnp.bfloat16),
            jax.ShapeDtypeStruct((events_dev, features), jnp.bfloat16),
        ),
        in_specs=[vmem] * 7,
        out_specs=(vmem,) * 3,
        scratch_shapes=[
            pltpu.VMEM((ctx // 2, 2 * lat_dev, width), jnp.float32),
            pltpu.VMEM((ctx // 2, 2 * lat_dev, features), jnp.float32),
            pltpu.VMEM((ctx - first_block, events_dev, lanes), jnp.float32),
            pltpu.VMEM((ctx, events_dev, lanes), jnp.bfloat16),
        ],
        compiler_params=params(24),
        name="grads",
    )(probs, used_keys, used_values, proj, wide_q, row_pair, row_far)


def solution(mesh):
    in_specs = (
        P("ctx", None),
        P("ctx", None),
        P(),
        P(None, "hd"),
        P("hd", None),
        P("hd", "ctx"),
        P("ctx", "hd"),
        P("ctx", "hd"),
        P("ctx", "hd"),
        P(),
        P(),
    )
    out_specs = (P("ctx", "hd"), P("ctx", "hd"), P("ctx", "hd"))
    ctx, hd = mesh.shape["ctx"], mesh.shape["hd"]

    def per_device(*arrays):
        lat_dev, features = arrays[6].shape
        fits = ctx * arrays[7].size * arrays[7].dtype.itemsize <= 2 * 1024 * 1024
        powers = ctx == 8 and hd >= 2 and ctx & (ctx - 1) == 0 and hd & (hd - 1) == 0
        aligned = 2 * lat_dev == 8 and features % HDIM == 0 and lat_dev <= Q_ROWS
        if fits and powers and aligned:
            return per_device_packed(*arrays)
        return per_device_streamed(*arrays)

    return jax.shard_map(
        per_device, mesh=mesh, in_specs=in_specs, out_specs=out_specs, check_vma=False
    )
```

```python
import functools
import math

import jax
import jax.numpy as jnp
from jax import lax
from jax.experimental import pallas as pl
from jax.experimental.pallas import tpu as pltpu
from jax.sharding import PartitionSpec as P

HDIM = 64
WINDOW = 256


def joined(value, axis, join):
    pieces = jax.tree.map(lambda part: lax.all_gather(part, axis), value)
    head = jax.tree.map(lambda part: part[0], pieces)
    tail = jax.tree.map(lambda part: part[1:], pieces)
    total, _ = lax.scan(lambda total, slab: (join(total, slab), None), head, tail)
    return total


def gelu_slope(values_in):
    inner = 0.7978845608028654 * (values_in + 0.044715 * values_in * values_in * values_in)
    tangent = jnp.tanh(inner)
    return 0.5 * (1.0 + tangent) + 0.5 * values_in * (
        1.0 - tangent * tangent
    ) * 0.7978845608028654 * (1.0 + 0.134145 * values_in * values_in)


def combine_totals(earlier, later):
    top_first, total_first, weight_first = earlier
    top_second, total_second, weight_second = later
    top_joint = jnp.maximum(top_first, top_second)
    factor_first = jnp.exp(top_first - top_joint)
    factor_second = jnp.exp(top_second - top_joint)
    return (
        top_joint,
        total_first * factor_first + total_second * factor_second,
        weight_first * factor_first + weight_second * factor_second,
    )


def per_device_streamed(
    cot, resid, norm_gain, w_in, w_out, w_proj, queries, keys, values, latent_pos, seg_start
):
    contract_last = (((1,), (1,)), ((), ()))
    rows_f32 = resid.astype(jnp.float32)
    inv_rms = lax.rsqrt(jnp.mean(rows_f32 * rows_f32, axis=-1, keepdims=True) + 1e-05)
    gain_f32 = norm_gain.astype(jnp.float32)
    normed = (rows_f32 * inv_rms * gain_f32).astype(jnp.bfloat16)
    pre_act = jnp.dot(normed, w_in, preferred_element_type=jnp.float32)
    hidden_grad = lax.dot_general(cot, w_out, contract_last, preferred_element_type=jnp.float32)
    pre_grad = (hidden_grad * gelu_slope(pre_act)).astype(jnp.bfloat16)
    partial_grad = lax.dot_general(
        pre_grad, w_in, contract_last, preferred_element_type=jnp.float32
    )
    whole_proj = lax.all_gather(w_proj, "ctx", axis=1, tiled=True)
    normed_grad = lax.psum(partial_grad, "hd")
    weighted = normed_grad * gain_f32
    unit_rows = rows_f32 * inv_rms
    resid_grad = (
        cot.astype(jnp.float32)
        + inv_rms * (weighted - unit_rows * jnp.mean(weighted * unit_rows, axis=-1, keepdims=True))
    ).astype(jnp.bfloat16)
    out_grad = lax.dot_general(
        resid_grad, whole_proj, contract_last, preferred_element_type=jnp.float32
    ).astype(jnp.bfloat16)
    all_queries, all_grads = (
        lax.all_gather(queries, "ctx", axis=0, tiled=True),
        lax.all_gather(out_grad, "ctx", axis=0, tiled=True),
    )
    ctx_count = lax.axis_size("ctx")
    lat_dev = cot.shape[0]
    latents = lat_dev * ctx_count
    blocks = max(1, min(lat_dev, latents // 512))
    per_block = lat_dev // blocks
    block_rows = ctx_count * per_block
    features = queries.shape[1]
    local_heads = features // HDIM
    events_dev = keys.shape[0]
    event_index = lax.axis_index("ctx") * events_dev + jnp.arange(events_dev, dtype=jnp.int32)
    factor = 1.0 / math.sqrt(HDIM)
    head_keys = keys.reshape(events_dev, local_heads, HDIM)
    head_values = values.reshape(events_dev, local_heads, HDIM)

    def block_view(array, which):
        shaped = array.reshape((ctx_count, blocks, per_block) + array.shape[1:])
        picked = lax.dynamic_index_in_dim(shaped, which, 1, keepdims=False)
        return picked.reshape((block_rows,) + array.shape[1:])

    def block_terms(which):
        block_q = block_view(all_queries, which).reshape(block_rows, local_heads, HDIM)
        block_do = block_view(all_grads, which).reshape(block_rows, local_heads, HDIM)
        block_pos = block_view(latent_pos, which)
        block_start = block_view(seg_start, which)
        visible = (event_index[None, :] >= block_start[:, None]) & (
            event_index[None, :] <= block_pos[:, None]
        )
        scores = factor * jnp.einsum(
            "rhe,khe->hrk", block_q, head_keys, preferred_element_type=jnp.float32
        )
        prob_grad = jnp.einsum(
            "rhe,khe->hrk", block_do, head_values, preferred_element_type=jnp.float32
        )
        return (block_q, block_do, visible[None], scores, prob_grad)

    def first_pass(carry, which):
        block_q, block_do, visible, scores, prob_grad = block_terms(which)
        block_top = jnp.max(jnp.where(visible, scores, -1e30), axis=2)
        expo = jnp.where(visible, jnp.exp(scores - block_top[..., None]), 0.0)
        return (carry, (block_top, jnp.sum(expo, axis=2), jnp.sum(expo * prob_grad, axis=2)))

    unused, local_totals = lax.scan(first_pass, jnp.int32(0), jnp.arange(blocks, dtype=jnp.int32))
    tops, totals, weight_sums = joined(local_totals, "ctx", combine_totals)
    deltas = weight_sums / totals

    def second_pass(carry, which):
        key_acc, value_acc = carry
        block_q, block_do, visible, scores, prob_grad = block_terms(which)
        block_top = lax.dynamic_index_in_dim(tops, which, 0, keepdims=False)
        block_total = lax.dynamic_index_in_dim(totals, which, 0, keepdims=False)
        block_delta = lax.dynamic_index_in_dim(deltas, which, 0, keepdims=False)
        expo = jnp.where(visible, jnp.exp(scores - block_top[..., None]), 0.0)
        probs = expo / block_total[..., None]
        prob_round = probs.astype(jnp.bfloat16)
        score_grad = (factor * probs * (prob_grad - block_delta[..., None])).astype(jnp.bfloat16)
        value_acc = value_acc + jnp.einsum(
            "hrk,rhe->khe", prob_round, block_do, preferred_element_type=jnp.float32
        )
        key_acc = key_acc + jnp.einsum(
            "hrk,rhe->khe", score_grad, block_q, preferred_element_type=jnp.float32
        )
        query_part = jnp.einsum(
            "hrk,khe->rhe", score_grad, head_keys, preferred_element_type=jnp.float32
        )
        query_part = query_part.reshape(ctx_count, per_block, features)
        return ((key_acc, value_acc), query_part)

    start_acc = (
        jnp.zeros((events_dev, local_heads, HDIM), jnp.float32),
        jnp.zeros((events_dev, local_heads, HDIM), jnp.float32),
    )
    (key_acc, value_acc), query_parts = lax.scan(
        second_pass, start_acc, jnp.arange(blocks, dtype=jnp.int32)
    )
    query_parts = lax.psum_scatter(query_parts, "ctx", scatter_dimension=1, tiled=True)
    query_grad = query_parts.reshape(lat_dev, features).astype(jnp.bfloat16)
    key_grad = key_acc.reshape(events_dev, features).astype(jnp.bfloat16)
    value_grad = value_acc.reshape(events_dev, features).astype(jnp.bfloat16)
    return (query_grad, key_grad, value_grad)


NT = (((1,), (1,)), ((), ()))
TN = (((0,), (0,)), ((), ()))
Q_ROWS = 16
LATE_ROWS = 96
MLP_PARTS = 2


def load_kernel(
    k_ref,
    v_ref,
    w_ref,
    q_ref,
    cot_ref,
    resid_ref,
    gain_ref,
    pos_ref,
    start_ref,
    pack_ref,
    rows_ref,
    marks_ref,
    q_own,
    cot_own,
    resid_own,
    gain_own,
    pos_own,
    start_own,
    sems,
):
    events, half, cols = k_ref.shape[0], w_ref.shape[0] // 2, w_ref.shape[1]
    base = 2 * events
    moves = [
        (q_ref, q_own),
        (cot_ref, cot_own),
        (resid_ref, resid_own),
        (gain_ref, gain_own),
        (pos_ref, pos_own),
        (start_ref, start_own),
        (k_ref, pack_ref.at[pl.ds(0, events)]),
        (v_ref, pack_ref.at[pl.ds(events, events)]),
        (w_ref.at[pl.ds(0, half)], pack_ref.at[pl.ds(base, half), pl.ds(0, cols)]),
        (w_ref.at[pl.ds(half, half)], pack_ref.at[pl.ds(base, half), pl.ds(cols, cols)]),
    ]
    copies = [
        pltpu.make_async_copy(source, target, sems.at[slot])
        for slot, (source, target) in enumerate(moves)
    ]
    for copy in copies:
        copy.start()
    for copy in copies[:6]:
        copy.wait()
    rows = q_own[...].astype(jnp.float32)
    spare = jnp.zeros((Q_ROWS - rows.shape[0], rows.shape[1]), jnp.float32)
    pack_ref[base + half :, :] = jnp.concatenate([rows, spare], axis=0).astype(jnp.bfloat16)
    gain = gain_own[...].astype(jnp.float32).reshape(1, gain_own.shape[0])
    lat_dev = cot_own.shape[0]
    held = [cot_own[...].astype(jnp.float32), resid_own[...].astype(jnp.float32)]
    held += [jnp.broadcast_to(gain, (rows_ref.shape[0] - 2 * lat_dev, gain.shape[1]))]
    rows_ref[...] = jnp.concatenate(held, axis=0).astype(jnp.bfloat16)
    latents = pos_ref.shape[0]
    lane = lax.broadcasted_iota(jnp.int32, marks_ref.shape, 1) % latents
    first = lax.broadcasted_iota(jnp.int32, marks_ref.shape, 0) == 0
    marks = jnp.zeros(marks_ref.shape, jnp.int32)
    for latent in range(latents):
        pair = jnp.where(first, pos_own[latent], start_own[latent])
        marks = jnp.where(lane == latent, pair, marks)
    marks_ref[...] = marks
    for copy in copies[6:]:
        copy.wait()


def chip_rows(own_ref, other_ref):
    own, other = own_ref[...].astype(jnp.float32), other_ref[...].astype(jnp.float32)
    first = lax.axis_index("ctx") % 2 == 0
    low, high = jnp.where(first, own, other), jnp.where(first, other, own)
    half = own.shape[0] // 4
    cot = jnp.concatenate([low[:half], high[:half]], axis=0)
    rows = jnp.concatenate([low[half : 2 * half], high[half : 2 * half]], axis=0)
    return cot, rows, own[2 * half : 2 * half + 1]


def rms_parts(rows):
    inv_rms = lax.rsqrt(jnp.mean(rows * rows, axis=-1, keepdims=True) + 1e-05)
    return inv_rms, rows * inv_rms


def mlp_kernel(own_ref, other_ref, w_in_ref, w_out_ref, out_ref, w_in, sems):
    parts, size = w_in.shape[0], w_in.shape[2]
    copies = []
    for part in range(parts):
        span = pl.ds(part * size, size)
        copies.append(pltpu.make_async_copy(w_in_ref.at[:, span], w_in.at[part], sems.at[part]))
    for copy in copies:
        copy.start()
    cot, rows, gain = chip_rows(own_ref, other_ref)
    normed = (rms_parts(rows)[1] * gain).astype(jnp.bfloat16)
    hidden_grad = lax.dot_general(
        cot.astype(jnp.bfloat16), w_out_ref[...], NT, preferred_element_type=jnp.float32
    )
    total = jnp.zeros(out_ref.shape, jnp.float32)
    for part, copy in enumerate(copies):
        copy.wait()
        up = w_in[part]
        pre_act = jnp.dot(normed, up, preferred_element_type=jnp.float32)
        span = slice(part * size, (part + 1) * size)
        pre_grad = (hidden_grad[:, span] * gelu_slope(pre_act)).astype(jnp.bfloat16)
        total += lax.dot_general(pre_grad, up, NT, preferred_element_type=jnp.float32)
    out_ref[...] = total


def resid_kernel(part_ref, arrived_ref, own_ref, other_ref, out_ref):
    cot, rows, gain = chip_rows(own_ref, other_ref)
    inv_rms, unit = rms_parts(rows)
    weighted = (part_ref[...] + arrived_ref[...]) * gain
    grad = cot + inv_rms * (weighted - unit * jnp.mean(weighted * unit, axis=-1, keepdims=True))
    out_ref[...] = grad.astype(jnp.bfloat16)


def wide_rows(array, latents):
    features = array.shape[1]
    heads = features // HDIM
    shape = (heads * latents, features)
    row_head = lax.broadcasted_iota(jnp.int32, shape, 0) // latents
    own_head = row_head == lax.broadcasted_iota(jnp.int32, shape, 1) // HDIM
    return jnp.where(own_head, jnp.concatenate([array] * heads, axis=0), 0.0), own_head


def straight(index):
    return (index ^ (index >> 1) ^ (index >> 2)) % 2 == 0


def probs_kernel(offsets, latents, lat_dev, events_dev, first_block, *refs):
    marks_ref = refs[0]
    pack_refs = refs[1:-6]
    probs_ref, keys_ref, values_ref, proj_ref, wide_ref, q_all = refs[-6:]
    me = lax.axis_index("ctx")
    even = me % 2 == 0
    base = 2 * events_dev
    pack_rows = base + proj_ref.shape[1] + Q_ROWS
    places = []
    for ref, pair in zip(pack_refs, offsets):
        for slot, offset in enumerate(pair):
            places.append((ref, slot * pack_rows, offset))
    queries = {}
    for ref, row, offset in places:
        block = me ^ jnp.where(straight(me), *offset)
        proj_ref[block] = ref[row + base : row + base + proj_ref.shape[1], :]
        queries[offset] = ref[row + pack_rows - Q_ROWS : row + pack_rows, :].astype(jnp.float32)

        @pl.when(block >= first_block)
        def _(ref=ref, row=row, block=block):
            keys_ref[block - first_block] = ref[row : row + events_dev, :]
            values_ref[block - first_block] = ref[row + events_dev : row + base, :]

    for offset, own in queries.items():
        if offset[0] % 2 == 0:
            other = queries[(offset[0] ^ 1, offset[1] ^ 1)]
            low, high = jnp.where(even, own, other), jnp.where(even, other, own)
            chip = (me ^ jnp.where(straight(me), *offset)) // 2
            q_all[chip] = jnp.concatenate([low[:lat_dev], high[:lat_dev]], axis=0)
    wide_q = wide_rows(q_all[...].reshape(latents, q_all.shape[2]), latents)[0]
    wide_q = wide_q * (1.0 / math.sqrt(HDIM))
    wide_ref[...] = wide_q.astype(jnp.bfloat16)
    wide_qt = wide_q.T.astype(jnp.bfloat16)
    lanes = wide_qt.shape[1]

    pos, start = marks_ref[0:1, :], marks_ref[1:2, :]
    used, features = keys_ref.shape[0], keys_ref.shape[2]
    top = jnp.full((1, lanes), -1e30, jnp.float32)
    for slot in range(used):
        scores = jnp.dot(keys_ref[slot], wide_qt, preferred_element_type=jnp.float32)
        spot = (first_block + slot) * events_dev + lax.broadcasted_iota(jnp.int32, scores.shape, 0)
        scores = jnp.where((spot >= start) & (spot <= pos), scores, -1e30)
        probs_ref[first_block + slot] = scores
        top = jnp.maximum(top, jnp.max(scores, axis=0, keepdims=True))
    total = jnp.zeros((1, lanes), jnp.float32)
    for slot in range(used):
        expo = jnp.exp(probs_ref[first_block + slot] - top)
        probs_ref[first_block + slot] = expo
        total += jnp.sum(expo, axis=0, keepdims=True)
    share = 1.0 / total
    for slot in range(used):
        probs_ref[first_block + slot] = probs_ref[first_block + slot] * share
    probs_ref[:first_block] = jnp.zeros((first_block, events_dev, lanes), jnp.float32)


def grads_kernel(
    row_offsets,
    pair_offset,
    latents,
    first_block,
    probs_ref,
    keys_ref,
    values_ref,
    proj_ref,
    wide_ref,
    *refs,
):
    row_refs = refs[: len(row_offsets)]
    qg_ref, kg_ref, vg_ref, rows_all, qg_all, grad_all, scores_all = refs[len(row_offsets) :]
    me = lax.axis_index("ctx")
    lat_dev = qg_ref.shape[0]
    blocks, events_dev, lanes = probs_ref.shape
    used, features = keys_ref.shape[0], keys_ref.shape[2]
    factor = 1.0 / math.sqrt(HDIM)
    for offset, ref in zip(row_offsets, row_refs):
        pair = ref[...].astype(jnp.float32)
        chip = (me // 2) ^ jnp.where(straight(me), *offset)
        rows_all[chip] = pair[: 2 * lat_dev]
        rows_all[chip ^ jnp.where(straight(me), *pair_offset)] = pair[2 * lat_dev :]
    resid_grad = rows_all[...].reshape(latents, rows_all.shape[2]).astype(jnp.bfloat16)
    cols = features // 2
    upper = jnp.concatenate([proj_ref[block, :, :cols] for block in range(blocks)], axis=1)
    lower = jnp.concatenate([proj_ref[block, :, cols:] for block in range(blocks)], axis=1)
    out_grad = [
        lax.dot_general(resid_grad, piece, NT, preferred_element_type=jnp.float32)
        for piece in (upper, lower)
    ]
    out_grad = jnp.concatenate(out_grad, axis=1).astype(jnp.bfloat16).astype(jnp.float32)
    wide_g, own_head = wide_rows(out_grad, latents)
    wide_gt, wide_g = wide_g.T.astype(jnp.bfloat16), wide_g.astype(jnp.bfloat16)
    delta = jnp.zeros((1, lanes), jnp.float32)
    for slot in range(used):
        prob_grad = jnp.dot(values_ref[slot], wide_gt, preferred_element_type=jnp.float32)
        grad_all[slot] = prob_grad
        delta += jnp.sum(probs_ref[first_block + slot] * prob_grad, axis=0, keepdims=True)
    wide = jnp.zeros((lanes, features), jnp.float32)
    for slot in range(used):
        score_grad = probs_ref[first_block + slot] * (grad_all[slot] - delta)
        score_grad = score_grad.astype(jnp.bfloat16)
        scores_all[first_block + slot] = score_grad
        wide += lax.dot_general(
            score_grad, keys_ref[slot], TN, preferred_element_type=jnp.float32
        )
    for slot in range(first_block):
        scores_all[slot] = jnp.zeros((events_dev, lanes), jnp.bfloat16)
    wide = jnp.where(own_head, wide, 0.0)
    total = sum(wide[head * latents : (head + 1) * latents] for head in range(lanes // latents))
    qg_all[...] = total.reshape(qg_all.shape)
    pair = qg_all[me // 2]
    mine = jnp.where(me % 2 == 0, pair[:lat_dev], pair[lat_dev:])
    qg_ref[...] = (factor * mine).astype(jnp.bfloat16)
    prob_round = probs_ref[me].astype(jnp.bfloat16)
    vg_ref[...] = jnp.dot(prob_round, wide_g, preferred_element_type=jnp.float32).astype(
        jnp.bfloat16
    )
    kg_ref[...] = jnp.dot(scores_all[me], wide_ref[...], preferred_element_type=jnp.float32).astype(
        jnp.bfloat16
    )


def swap(array, bit, other_bit=None):
    bits = (bit, bit if other_bit is None else other_bit)
    pairs = [(c, c ^ bits[c.bit_count() % 2]) for c in range(lax.axis_size("ctx"))]
    return lax.ppermute(array, "ctx", pairs)


def swap_hd(array, bit):
    ctx, hd = lax.axis_size("ctx"), lax.axis_size("hd")
    pairs = [
        (c * hd + z, (c ^ 1) * hd + (z ^ bit)) for c in range(ctx) for z in range(hd)
    ]
    return lax.ppermute(array, ("ctx", "hd"), pairs)


def after(array, *others):
    return lax.optimization_barrier((array, *others))[0]


def in_hbm(array):
    return pltpu.with_memory_space_constraint(array, pltpu.HBM)


def params(mebibytes):
    return pltpu.CompilerParams(vmem_limit_bytes=mebibytes * 1024 * 1024)


def per_device_packed(
    cot, resid, norm_gain, w_in, w_out, w_proj, queries, keys, values, latent_pos, seg_start
):
    ctx, hd = lax.axis_size("ctx"), lax.axis_size("hd")
    lat_dev, width = cot.shape
    latents = lat_dev * ctx
    events_dev, features = keys.shape
    hidden = w_in.shape[1]
    vmem = pl.BlockSpec(memory_space=pltpu.VMEM)
    hbm = pl.BlockSpec(memory_space=pltpu.HBM)
    pack_rows = 2 * events_dev + w_proj.shape[0] // 2 + Q_ROWS
    lanes = features // HDIM * latents
    pack, own_rows, marks = pl.pallas_call(
        load_kernel,
        out_shape=(
            jax.ShapeDtypeStruct((pack_rows, features), jnp.bfloat16),
            jax.ShapeDtypeStruct((4 * lat_dev, width), jnp.bfloat16),
            jax.ShapeDtypeStruct((8, lanes), jnp.int32),
        ),
        in_specs=[hbm] * 9,
        out_specs=(vmem,) * 3,
        scratch_shapes=[
            pltpu.VMEM((lat_dev, features), jnp.bfloat16),
            pltpu.VMEM((lat_dev, width), jnp.bfloat16),
            pltpu.VMEM((lat_dev, width), jnp.bfloat16),
            pltpu.VMEM((width,), jnp.bfloat16),
            pltpu.SMEM((latents,), jnp.int32),
            pltpu.SMEM((latents,), jnp.int32),
            pltpu.SemaphoreType.DMA((10,)),
        ],
        compiler_params=params(8),
        name="load",
    )(
        *[
            in_hbm(array)
            for array in (
                keys, values, w_proj, queries, cot, resid, norm_gain, latent_pos, seg_start
            )
        ]
    )
    other_rows = swap(own_rows, 1)
    near_out = swap(w_out, 1)

    chip_bits = [1 << shift for shift in range(1, ctx.bit_length() - 1)]
    hd_bits = [1 << shift for shift in range(hd.bit_length() - 1)]
    steps = (tuple(bit | 1 for bit in chip_bits), tuple(bit | 1 for bit in reversed(chip_bits)))
    first_piece = swap(pack, *steps[0])
    part = pl.pallas_call(
        mlp_kernel,
        out_shape=jax.ShapeDtypeStruct((2 * lat_dev, width), jnp.float32),
        in_specs=[vmem] * 2 + [hbm, vmem],
        out_specs=vmem,
        scratch_shapes=[
            pltpu.VMEM((MLP_PARTS, width, hidden // MLP_PARTS), jnp.bfloat16),
            pltpu.SemaphoreType.DMA((MLP_PARTS,)),
        ],
        compiler_params=params(16),
        cost_estimate=pl.CostEstimate(
            flops=12 * lat_dev * w_in.size, bytes_accessed=4 * w_in.size, transcendentals=0
        ),
        name="mlp",
    )(own_rows, other_rows, in_hbm(w_in), near_out)
    first_pair = jnp.concatenate([pack, after(first_piece, part)], axis=0)
    second_pair = swap(first_pair, *steps[1])
    for bit in hd_bits[:-1]:
        part = part + swap_hd(part, bit)
    early_rows = first_pair.shape[0] - LATE_ROWS
    early_other = swap(after(first_pair, part)[:early_rows], 1)
    late_other = swap(after(first_pair, part)[early_rows:], 1)
    first_other = jnp.concatenate([early_other, late_other], axis=0)
    arrived = swap_hd(part, hd_bits[-1])
    arrived = after(arrived, early_other)
    rows = pl.pallas_call(
        resid_kernel,
        out_shape=jax.ShapeDtypeStruct((2 * lat_dev, width), jnp.bfloat16),
        in_specs=[vmem] * 4,
        out_specs=vmem,
        compiler_params=params(8),
        name="resid",
    )(part, arrived, own_rows, other_rows)
    rows = after(rows, late_other)
    row_x = swap(rows, *steps[0])
    row_pair = jnp.concatenate([rows, row_x], axis=0)
    row_far = swap(row_pair, *steps[1])
    second_other = swap(after(second_pair, row_x), 1)

    corner = tuple(step ^ other for step, other in zip(*steps))
    turn = lambda pair: (pair[1] ^ 1, pair[0] ^ 1)
    near, far = [(0, 0), steps[0]], [steps[1], corner]
    offsets = [near, [turn(pair) for pair in near], far, [turn(pair) for pair in far]]
    first_block = max(0, events_dev * ctx // 2 - WINDOW) // events_dev
    lanes = features // HDIM * latents
    pair_offset = tuple(bit // 2 for bit in steps[0])
    row_offsets = [(0, 0), tuple(bit // 2 for bit in steps[1])]
    probs, used_keys, used_values, proj, wide_q = pl.pallas_call(
        functools.partial(probs_kernel, offsets, latents, lat_dev, events_dev, first_block),
        out_shape=(
            jax.ShapeDtypeStruct((ctx, events_dev, lanes), jnp.float32),
            jax.ShapeDtypeStruct((ctx - first_block, events_dev, features), jnp.bfloat16),
            jax.ShapeDtypeStruct((ctx - first_block, events_dev, features), jnp.bfloat16),
            jax.ShapeDtypeStruct((ctx, w_proj.shape[0] // 2, features), jnp.bfloat16),
            jax.ShapeDtypeStruct((lanes, features), jnp.bfloat16),
        ),
        in_specs=[vmem] * 5,
        out_specs=(vmem,) * 5,
        scratch_shapes=[pltpu.VMEM((ctx // 2, 2 * lat_dev, features), jnp.float32)],
        compiler_params=params(24),
        cost_estimate=pl.CostEstimate(
            flops=2 * ctx * keys.size * lanes, bytes_accessed=8 * keys.size, transcendentals=0
        ),
        name="probs",
    )(marks, first_pair, first_other, second_pair, second_other)
    return pl.pallas_call(
        functools.partial(
            grads_kernel, row_offsets, pair_offset, latents, first_block
        ),
        out_shape=(
            jax.ShapeDtypeStruct((lat_dev, features), jnp.bfloat16),
            jax.ShapeDtypeStruct((events_dev, features), jnp.bfloat16),
            jax.ShapeDtypeStruct((events_dev, features), jnp.bfloat16),
        ),
        in_specs=[vmem] * 7,
        out_specs=(vmem,) * 3,
        scratch_shapes=[
            pltpu.VMEM((ctx // 2, 2 * lat_dev, width), jnp.float32),
            pltpu.VMEM((ctx // 2, 2 * lat_dev, features), jnp.float32),
            pltpu.VMEM((ctx - first_block, events_dev, lanes), jnp.float32),
            pltpu.VMEM((ctx, events_dev, lanes), jnp.bfloat16),
        ],
        compiler_params=params(24),
        name="grads",
    )(probs, used_keys, used_values, proj, wide_q, row_pair, row_far)


def solution(mesh):
    in_specs = (
        P("ctx", None),
        P("ctx", None),
        P(),
        P(None, "hd"),
        P("hd", None),
        P("hd", "ctx"),
        P("ctx", "hd"),
        P("ctx", "hd"),
        P("ctx", "hd"),
        P(),
        P(),
    )
    out_specs = (P("ctx", "hd"), P("ctx", "hd"), P("ctx", "hd"))
    ctx, hd = mesh.shape["ctx"], mesh.shape["hd"]

    def per_device(*arrays):
        lat_dev, features = arrays[6].shape
        fits = ctx * arrays[7].size * arrays[7].dtype.itemsize <= 2 * 1024 * 1024
        powers = ctx == 8 and hd >= 2 and ctx & (ctx - 1) == 0 and hd & (hd - 1) == 0
        aligned = 2 * lat_dev == 8 and features % HDIM == 0 and lat_dev <= Q_ROWS
        if fits and powers and aligned:
            return per_device_packed(*arrays)
        return per_device_streamed(*arrays)

    return jax.shard_map(
        per_device, mesh=mesh, in_specs=in_specs, out_specs=out_specs, check_vma=False
    )
```

```python
import functools
import math

import jax
import jax.numpy as jnp
from jax import lax
from jax.experimental import pallas as pl
from jax.experimental.pallas import tpu as pltpu
from jax.sharding import PartitionSpec as P

HDIM = 64
WINDOW = 256


def joined(value, axis, join):
    pieces = jax.tree.map(lambda part: lax.all_gather(part, axis), value)
    head = jax.tree.map(lambda part: part[0], pieces)
    tail = jax.tree.map(lambda part: part[1:], pieces)
    total, _ = lax.scan(lambda total, slab: (join(total, slab), None), head, tail)
    return total


def gelu_slope(values_in):
    inner = 0.7978845608028654 * (values_in + 0.044715 * values_in * values_in * values_in)
    tangent = jnp.tanh(inner)
    return 0.5 * (1.0 + tangent) + 0.5 * values_in * (
        1.0 - tangent * tangent
    ) * 0.7978845608028654 * (1.0 + 0.134145 * values_in * values_in)


def combine_totals(earlier, later):
    top_first, total_first, weight_first = earlier
    top_second, total_second, weight_second = later
    top_joint = jnp.maximum(top_first, top_second)
    factor_first = jnp.exp(top_first - top_joint)
    factor_second = jnp.exp(top_second - top_joint)
    return (
        top_joint,
        total_first * factor_first + total_second * factor_second,
        weight_first * factor_first + weight_second * factor_second,
    )


def per_device_streamed(
    cot, resid, norm_gain, w_in, w_out, w_proj, queries, keys, values, latent_pos, seg_start
):
    contract_last = (((1,), (1,)), ((), ()))
    rows_f32 = resid.astype(jnp.float32)
    inv_rms = lax.rsqrt(jnp.mean(rows_f32 * rows_f32, axis=-1, keepdims=True) + 1e-05)
    gain_f32 = norm_gain.astype(jnp.float32)
    normed = (rows_f32 * inv_rms * gain_f32).astype(jnp.bfloat16)
    pre_act = jnp.dot(normed, w_in, preferred_element_type=jnp.float32)
    hidden_grad = lax.dot_general(cot, w_out, contract_last, preferred_element_type=jnp.float32)
    pre_grad = (hidden_grad * gelu_slope(pre_act)).astype(jnp.bfloat16)
    partial_grad = lax.dot_general(
        pre_grad, w_in, contract_last, preferred_element_type=jnp.float32
    )
    whole_proj = lax.all_gather(w_proj, "ctx", axis=1, tiled=True)
    normed_grad = lax.psum(partial_grad, "hd")
    weighted = normed_grad * gain_f32
    unit_rows = rows_f32 * inv_rms
    resid_grad = (
        cot.astype(jnp.float32)
        + inv_rms * (weighted - unit_rows * jnp.mean(weighted * unit_rows, axis=-1, keepdims=True))
    ).astype(jnp.bfloat16)
    out_grad = lax.dot_general(
        resid_grad, whole_proj, contract_last, preferred_element_type=jnp.float32
    ).astype(jnp.bfloat16)
    all_queries, all_grads = (
        lax.all_gather(queries, "ctx", axis=0, tiled=True),
        lax.all_gather(out_grad, "ctx", axis=0, tiled=True),
    )
    ctx_count = lax.axis_size("ctx")
    lat_dev = cot.shape[0]
    latents = lat_dev * ctx_count
    blocks = max(1, min(lat_dev, latents // 512))
    per_block = lat_dev // blocks
    block_rows = ctx_count * per_block
    features = queries.shape[1]
    local_heads = features // HDIM
    events_dev = keys.shape[0]
    event_index = lax.axis_index("ctx") * events_dev + jnp.arange(events_dev, dtype=jnp.int32)
    factor = 1.0 / math.sqrt(HDIM)
    head_keys = keys.reshape(events_dev, local_heads, HDIM)
    head_values = values.reshape(events_dev, local_heads, HDIM)

    def block_view(array, which):
        shaped = array.reshape((ctx_count, blocks, per_block) + array.shape[1:])
        picked = lax.dynamic_index_in_dim(shaped, which, 1, keepdims=False)
        return picked.reshape((block_rows,) + array.shape[1:])

    def block_terms(which):
        block_q = block_view(all_queries, which).reshape(block_rows, local_heads, HDIM)
        block_do = block_view(all_grads, which).reshape(block_rows, local_heads, HDIM)
        block_pos = block_view(latent_pos, which)
        block_start = block_view(seg_start, which)
        visible = (event_index[None, :] >= block_start[:, None]) & (
            event_index[None, :] <= block_pos[:, None]
        )
        scores = factor * jnp.einsum(
            "rhe,khe->hrk", block_q, head_keys, preferred_element_type=jnp.float32
        )
        prob_grad = jnp.einsum(
            "rhe,khe->hrk", block_do, head_values, preferred_element_type=jnp.float32
        )
        return (block_q, block_do, visible[None], scores, prob_grad)

    def first_pass(carry, which):
        block_q, block_do, visible, scores, prob_grad = block_terms(which)
        block_top = jnp.max(jnp.where(visible, scores, -1e30), axis=2)
        expo = jnp.where(visible, jnp.exp(scores - block_top[..., None]), 0.0)
        return (carry, (block_top, jnp.sum(expo, axis=2), jnp.sum(expo * prob_grad, axis=2)))

    unused, local_totals = lax.scan(first_pass, jnp.int32(0), jnp.arange(blocks, dtype=jnp.int32))
    tops, totals, weight_sums = joined(local_totals, "ctx", combine_totals)
    deltas = weight_sums / totals

    def second_pass(carry, which):
        key_acc, value_acc = carry
        block_q, block_do, visible, scores, prob_grad = block_terms(which)
        block_top = lax.dynamic_index_in_dim(tops, which, 0, keepdims=False)
        block_total = lax.dynamic_index_in_dim(totals, which, 0, keepdims=False)
        block_delta = lax.dynamic_index_in_dim(deltas, which, 0, keepdims=False)
        expo = jnp.where(visible, jnp.exp(scores - block_top[..., None]), 0.0)
        probs = expo / block_total[..., None]
        prob_round = probs.astype(jnp.bfloat16)
        score_grad = (factor * probs * (prob_grad - block_delta[..., None])).astype(jnp.bfloat16)
        value_acc = value_acc + jnp.einsum(
            "hrk,rhe->khe", prob_round, block_do, preferred_element_type=jnp.float32
        )
        key_acc = key_acc + jnp.einsum(
            "hrk,rhe->khe", score_grad, block_q, preferred_element_type=jnp.float32
        )
        query_part = jnp.einsum(
            "hrk,khe->rhe", score_grad, head_keys, preferred_element_type=jnp.float32
        )
        query_part = query_part.reshape(ctx_count, per_block, features)
        return ((key_acc, value_acc), query_part)

    start_acc = (
        jnp.zeros((events_dev, local_heads, HDIM), jnp.float32),
        jnp.zeros((events_dev, local_heads, HDIM), jnp.float32),
    )
    (key_acc, value_acc), query_parts = lax.scan(
        second_pass, start_acc, jnp.arange(blocks, dtype=jnp.int32)
    )
    query_parts = lax.psum_scatter(query_parts, "ctx", scatter_dimension=1, tiled=True)
    query_grad = query_parts.reshape(lat_dev, features).astype(jnp.bfloat16)
    key_grad = key_acc.reshape(events_dev, features).astype(jnp.bfloat16)
    value_grad = value_acc.reshape(events_dev, features).astype(jnp.bfloat16)
    return (query_grad, key_grad, value_grad)


NT = (((1,), (1,)), ((), ()))
TN = (((0,), (0,)), ((), ()))
Q_ROWS = 16
LATE_ROWS = 96


def load_kernel(
    k_ref,
    v_ref,
    w_ref,
    q_ref,
    cot_ref,
    resid_ref,
    gain_ref,
    pos_ref,
    start_ref,
    pack_ref,
    rows_ref,
    marks_ref,
    q_own,
    cot_own,
    resid_own,
    gain_own,
    pos_own,
    start_own,
    sems,
):
    events, half, cols = k_ref.shape[0], w_ref.shape[0] // 2, w_ref.shape[1]
    base = 2 * events
    moves = [
        (q_ref, q_own),
        (cot_ref, cot_own),
        (resid_ref, resid_own),
        (gain_ref, gain_own),
        (pos_ref, pos_own),
        (start_ref, start_own),
        (k_ref, pack_ref.at[pl.ds(0, events)]),
        (v_ref, pack_ref.at[pl.ds(events, events)]),
        (w_ref.at[pl.ds(0, half)], pack_ref.at[pl.ds(base, half), pl.ds(0, cols)]),
        (w_ref.at[pl.ds(half, half)], pack_ref.at[pl.ds(base, half), pl.ds(cols, cols)]),
    ]
    copies = [
        pltpu.make_async_copy(source, target, sems.at[slot])
        for slot, (source, target) in enumerate(moves)
    ]
    for copy in copies:
        copy.start()
    for copy in copies[:6]:
        copy.wait()
    rows = q_own[...].astype(jnp.float32)
    spare = jnp.zeros((Q_ROWS - rows.shape[0], rows.shape[1]), jnp.float32)
    pack_ref[base + half :, :] = jnp.concatenate([rows, spare], axis=0).astype(jnp.bfloat16)
    gain = gain_own[...].astype(jnp.float32).reshape(1, gain_own.shape[0])
    lat_dev = cot_own.shape[0]
    held = [cot_own[...].astype(jnp.float32), resid_own[...].astype(jnp.float32)]
    held += [jnp.broadcast_to(gain, (rows_ref.shape[0] - 2 * lat_dev, gain.shape[1]))]
    rows_ref[...] = jnp.concatenate(held, axis=0).astype(jnp.bfloat16)
    latents = pos_ref.shape[0]
    lane = lax.broadcasted_iota(jnp.int32, marks_ref.shape, 1) % latents
    first = lax.broadcasted_iota(jnp.int32, marks_ref.shape, 0) == 0
    marks = jnp.zeros(marks_ref.shape, jnp.int32)
    for latent in range(latents):
        pair = jnp.where(first, pos_own[latent], start_own[latent])
        marks = jnp.where(lane == latent, pair, marks)
    marks_ref[...] = marks
    for copy in copies[6:]:
        copy.wait()


def chip_rows(own_ref, other_ref):
    own, other = own_ref[...].astype(jnp.float32), other_ref[...].astype(jnp.float32)
    first = lax.axis_index("ctx") % 2 == 0
    low, high = jnp.where(first, own, other), jnp.where(first, other, own)
    half = own.shape[0] // 4
    cot = jnp.concatenate([low[:half], high[:half]], axis=0)
    rows = jnp.concatenate([low[half : 2 * half], high[half : 2 * half]], axis=0)
    return cot, rows, own[2 * half : 2 * half + 1]


def rms_parts(rows):
    inv_rms = lax.rsqrt(jnp.mean(rows * rows, axis=-1, keepdims=True) + 1e-05)
    return inv_rms, rows * inv_rms


def fetch_kernel(w_in_ref, out_ref, sem):
    copy = pltpu.make_async_copy(w_in_ref, out_ref, sem)
    copy.start()
    copy.wait()


def mlp_kernel(own_ref, other_ref, w_in_ref, w_out_ref, out_ref):
    cot, rows, gain = chip_rows(own_ref, other_ref)
    normed = (rms_parts(rows)[1] * gain).astype(jnp.bfloat16)
    hidden_grad = lax.dot_general(
        cot.astype(jnp.bfloat16), w_out_ref[...], NT, preferred_element_type=jnp.float32
    )
    pre_act = jnp.dot(normed, w_in_ref[...], preferred_element_type=jnp.float32)
    pre_grad = (hidden_grad * gelu_slope(pre_act)).astype(jnp.bfloat16)
    out_ref[...] = lax.dot_general(pre_grad, w_in_ref[...], NT, preferred_element_type=jnp.float32)


def resid_kernel(part_ref, arrived_ref, own_ref, other_ref, out_ref):
    cot, rows, gain = chip_rows(own_ref, other_ref)
    inv_rms, unit = rms_parts(rows)
    weighted = (part_ref[...] + arrived_ref[...]) * gain
    grad = cot + inv_rms * (weighted - unit * jnp.mean(weighted * unit, axis=-1, keepdims=True))
    out_ref[...] = grad.astype(jnp.bfloat16)


def wide_rows(array, latents):
    features = array.shape[1]
    heads = features // HDIM
    shape = (heads * latents, features)
    row_head = lax.broadcasted_iota(jnp.int32, shape, 0) // latents
    own_head = row_head == lax.broadcasted_iota(jnp.int32, shape, 1) // HDIM
    return jnp.where(own_head, jnp.concatenate([array] * heads, axis=0), 0.0), own_head


def straight(index):
    return (index ^ (index >> 1) ^ (index >> 2)) % 2 == 0


def probs_kernel(offsets, latents, lat_dev, events_dev, first_block, *refs):
    marks_ref = refs[0]
    pack_refs = refs[1:-6]
    probs_ref, keys_ref, values_ref, proj_ref, wide_ref, q_all = refs[-6:]
    me = lax.axis_index("ctx")
    even = me % 2 == 0
    base = 2 * events_dev
    pack_rows = base + proj_ref.shape[1] + Q_ROWS
    places = []
    for ref, pair in zip(pack_refs, offsets):
        for slot, offset in enumerate(pair):
            places.append((ref, slot * pack_rows, offset))
    queries = {}
    for ref, row, offset in places:
        block = me ^ jnp.where(straight(me), *offset)
        proj_ref[block] = ref[row + base : row + base + proj_ref.shape[1], :]
        queries[offset] = ref[row + pack_rows - Q_ROWS : row + pack_rows, :].astype(jnp.float32)

        @pl.when(block >= first_block)
        def _(ref=ref, row=row, block=block):
            keys_ref[block - first_block] = ref[row : row + events_dev, :]
            values_ref[block - first_block] = ref[row + events_dev : row + base, :]

    for offset, own in queries.items():
        if offset[0] % 2 == 0:
            other = queries[(offset[0] ^ 1, offset[1] ^ 1)]
            low, high = jnp.where(even, own, other), jnp.where(even, other, own)
            chip = (me ^ jnp.where(straight(me), *offset)) // 2
            q_all[chip] = jnp.concatenate([low[:lat_dev], high[:lat_dev]], axis=0)
    wide_q = wide_rows(q_all[...].reshape(latents, q_all.shape[2]), latents)[0]
    wide_q = wide_q * (1.0 / math.sqrt(HDIM))
    wide_ref[...] = wide_q.astype(jnp.bfloat16)
    wide_qt = wide_q.T.astype(jnp.bfloat16)
    lanes = wide_qt.shape[1]

    pos, start = marks_ref[0:1, :], marks_ref[1:2, :]
    used, features = keys_ref.shape[0], keys_ref.shape[2]
    top = jnp.full((1, lanes), -1e30, jnp.float32)
    for slot in range(used):
        scores = jnp.dot(keys_ref[slot], wide_qt, preferred_element_type=jnp.float32)
        spot = (first_block + slot) * events_dev + lax.broadcasted_iota(jnp.int32, scores.shape, 0)
        scores = jnp.where((spot >= start) & (spot <= pos), scores, -1e30)
        probs_ref[first_block + slot] = scores
        top = jnp.maximum(top, jnp.max(scores, axis=0, keepdims=True))
    total = jnp.zeros((1, lanes), jnp.float32)
    for slot in range(used):
        expo = jnp.exp(probs_ref[first_block + slot] - top)
        probs_ref[first_block + slot] = expo
        total += jnp.sum(expo, axis=0, keepdims=True)
    share = 1.0 / total
    for slot in range(used):
        probs_ref[first_block + slot] = probs_ref[first_block + slot] * share
    probs_ref[:first_block] = jnp.zeros((first_block, events_dev, lanes), jnp.float32)


def grads_kernel(
    row_offsets,
    pair_offset,
    latents,
    first_block,
    probs_ref,
    keys_ref,
    values_ref,
    proj_ref,
    wide_ref,
    *refs,
):
    row_refs = refs[: len(row_offsets)]
    qg_ref, kg_ref, vg_ref, rows_all, qg_all, grad_all, scores_all = refs[len(row_offsets) :]
    me = lax.axis_index("ctx")
    lat_dev = qg_ref.shape[0]
    blocks, events_dev, lanes = probs_ref.shape
    used, features = keys_ref.shape[0], keys_ref.shape[2]
    factor = 1.0 / math.sqrt(HDIM)
    for offset, ref in zip(row_offsets, row_refs):
        pair = ref[...].astype(jnp.float32)
        chip = (me // 2) ^ jnp.where(straight(me), *offset)
        rows_all[chip] = pair[: 2 * lat_dev]
        rows_all[chip ^ jnp.where(straight(me), *pair_offset)] = pair[2 * lat_dev :]
    resid_grad = rows_all[...].reshape(latents, rows_all.shape[2]).astype(jnp.bfloat16)
    cols = features // 2
    upper = jnp.concatenate([proj_ref[block, :, :cols] for block in range(blocks)], axis=1)
    lower = jnp.concatenate([proj_ref[block, :, cols:] for block in range(blocks)], axis=1)
    out_grad = [
        lax.dot_general(resid_grad, piece, NT, preferred_element_type=jnp.float32)
        for piece in (upper, lower)
    ]
    out_grad = jnp.concatenate(out_grad, axis=1).astype(jnp.bfloat16).astype(jnp.float32)
    wide_g, own_head = wide_rows(out_grad, latents)
    wide_gt, wide_g = wide_g.T.astype(jnp.bfloat16), wide_g.astype(jnp.bfloat16)
    delta = jnp.zeros((1, lanes), jnp.float32)
    for slot in range(used):
        prob_grad = jnp.dot(values_ref[slot], wide_gt, preferred_element_type=jnp.float32)
        grad_all[slot] = prob_grad
        delta += jnp.sum(probs_ref[first_block + slot] * prob_grad, axis=0, keepdims=True)
    wide = jnp.zeros((lanes, features), jnp.float32)
    for slot in range(used):
        score_grad = probs_ref[first_block + slot] * (grad_all[slot] - delta)
        score_grad = score_grad.astype(jnp.bfloat16)
        scores_all[first_block + slot] = score_grad
        wide += lax.dot_general(
            score_grad, keys_ref[slot], TN, preferred_element_type=jnp.float32
        )
    for slot in range(first_block):
        scores_all[slot] = jnp.zeros((events_dev, lanes), jnp.bfloat16)
    wide = jnp.where(own_head, wide, 0.0)
    total = sum(wide[head * latents : (head + 1) * latents] for head in range(lanes // latents))
    qg_all[...] = total.reshape(qg_all.shape)
    pair = qg_all[me // 2]
    mine = jnp.where(me % 2 == 0, pair[:lat_dev], pair[lat_dev:])
    qg_ref[...] = (factor * mine).astype(jnp.bfloat16)
    prob_round = probs_ref[me].astype(jnp.bfloat16)
    vg_ref[...] = jnp.dot(prob_round, wide_g, preferred_element_type=jnp.float32).astype(
        jnp.bfloat16
    )
    kg_ref[...] = jnp.dot(scores_all[me], wide_ref[...], preferred_element_type=jnp.float32).astype(
        jnp.bfloat16
    )


def swap(array, bit, other_bit=None):
    bits = (bit, bit if other_bit is None else other_bit)
    pairs = [(c, c ^ bits[c.bit_count() % 2]) for c in range(lax.axis_size("ctx"))]
    return lax.ppermute(array, "ctx", pairs)


def swap_hd(array, bit):
    ctx, hd = lax.axis_size("ctx"), lax.axis_size("hd")
    pairs = [
        (c * hd + z, (c ^ 1) * hd + (z ^ bit)) for c in range(ctx) for z in range(hd)
    ]
    return lax.ppermute(array, ("ctx", "hd"), pairs)


def after(array, *others):
    return lax.optimization_barrier((array, *others))[0]


def in_hbm(array):
    return pltpu.with_memory_space_constraint(array, pltpu.HBM)


def params(mebibytes):
    return pltpu.CompilerParams(vmem_limit_bytes=mebibytes * 1024 * 1024)


def per_device_packed(
    cot, resid, norm_gain, w_in, w_out, w_proj, queries, keys, values, latent_pos, seg_start
):
    ctx, hd = lax.axis_size("ctx"), lax.axis_size("hd")
    lat_dev, width = cot.shape
    latents = lat_dev * ctx
    events_dev, features = keys.shape
    vmem = pl.BlockSpec(memory_space=pltpu.VMEM)
    hbm = pl.BlockSpec(memory_space=pltpu.HBM)
    pack_rows = 2 * events_dev + w_proj.shape[0] // 2 + Q_ROWS
    lanes = features // HDIM * latents
    pack, own_rows, marks = pl.pallas_call(
        load_kernel,
        out_shape=(
            jax.ShapeDtypeStruct((pack_rows, features), jnp.bfloat16),
            jax.ShapeDtypeStruct((4 * lat_dev, width), jnp.bfloat16),
            jax.ShapeDtypeStruct((8, lanes), jnp.int32),
        ),
        in_specs=[hbm] * 9,
        out_specs=(vmem,) * 3,
        scratch_shapes=[
            pltpu.VMEM((lat_dev, features), jnp.bfloat16),
            pltpu.VMEM((lat_dev, width), jnp.bfloat16),
            pltpu.VMEM((lat_dev, width), jnp.bfloat16),
            pltpu.VMEM((width,), jnp.bfloat16),
            pltpu.SMEM((latents,), jnp.int32),
            pltpu.SMEM((latents,), jnp.int32),
            pltpu.SemaphoreType.DMA((10,)),
        ],
        compiler_params=params(8),
        name="load",
    )(
        *[
            in_hbm(array)
            for array in (
                keys, values, w_proj, queries, cot, resid, norm_gain, latent_pos, seg_start
            )
        ]
    )
    other_rows = swap(own_rows, 1)
    near_out = swap(w_out, 1)

    chip_bits = [1 << shift for shift in range(1, ctx.bit_length() - 1)]
    hd_bits = [1 << shift for shift in range(hd.bit_length() - 1)]
    steps = (tuple(bit | 1 for bit in chip_bits), tuple(bit | 1 for bit in reversed(chip_bits)))
    first_piece = swap(pack, *steps[0])
    near_in = pl.pallas_call(
        fetch_kernel,
        out_shape=jax.ShapeDtypeStruct(w_in.shape, jnp.bfloat16),
        in_specs=[hbm],
        out_specs=vmem,
        scratch_shapes=[pltpu.SemaphoreType.DMA(())],
        compiler_params=params(8),
        name="fetch",
    )(in_hbm(after(w_in, own_rows)))
    part = pl.pallas_call(
        mlp_kernel,
        out_shape=jax.ShapeDtypeStruct((2 * lat_dev, width), jnp.float32),
        in_specs=[vmem] * 4,
        out_specs=vmem,
        compiler_params=params(16),
        cost_estimate=pl.CostEstimate(
            flops=12 * lat_dev * w_in.size, bytes_accessed=4 * w_in.size, transcendentals=0
        ),
        name="mlp",
    )(own_rows, other_rows, near_in, near_out)
    first_pair = jnp.concatenate([pack, after(first_piece, part)], axis=0)
    second_pair = swap(first_pair, *steps[1])
    for bit in hd_bits[:-1]:
        part = part + swap_hd(part, bit)
    early_rows = first_pair.shape[0] - LATE_ROWS
    early_other = swap(after(first_pair, part)[:early_rows], 1)
    late_other = swap(after(first_pair, part)[early_rows:], 1)
    first_other = jnp.concatenate([early_other, late_other], axis=0)
    arrived = swap_hd(part, hd_bits[-1])
    arrived = after(arrived, early_other)
    rows = pl.pallas_call(
        resid_kernel,
        out_shape=jax.ShapeDtypeStruct((2 * lat_dev, width), jnp.bfloat16),
        in_specs=[vmem] * 4,
        out_specs=vmem,
        compiler_params=params(8),
        name="resid",
    )(part, arrived, own_rows, other_rows)
    rows = after(rows, late_other)
    row_x = swap(rows, *steps[0])
    row_pair = jnp.concatenate([rows, row_x], axis=0)
    row_far = swap(row_pair, *steps[1])
    second_other = swap(after(second_pair, row_x), 1)

    corner = tuple(step ^ other for step, other in zip(*steps))
    turn = lambda pair: (pair[1] ^ 1, pair[0] ^ 1)
    near, far = [(0, 0), steps[0]], [steps[1], corner]
    offsets = [near, [turn(pair) for pair in near], far, [turn(pair) for pair in far]]
    first_block = max(0, events_dev * ctx // 2 - WINDOW) // events_dev
    lanes = features // HDIM * latents
    pair_offset = tuple(bit // 2 for bit in steps[0])
    row_offsets = [(0, 0), tuple(bit // 2 for bit in steps[1])]
    probs, used_keys, used_values, proj, wide_q = pl.pallas_call(
        functools.partial(probs_kernel, offsets, latents, lat_dev, events_dev, first_block),
        out_shape=(
            jax.ShapeDtypeStruct((ctx, events_dev, lanes), jnp.float32),
            jax.ShapeDtypeStruct((ctx - first_block, events_dev, features), jnp.bfloat16),
            jax.ShapeDtypeStruct((ctx - first_block, events_dev, features), jnp.bfloat16),
            jax.ShapeDtypeStruct((ctx, w_proj.shape[0] // 2, features), jnp.bfloat16),
            jax.ShapeDtypeStruct((lanes, features), jnp.bfloat16),
        ),
        in_specs=[vmem] * 5,
        out_specs=(vmem,) * 5,
        scratch_shapes=[pltpu.VMEM((ctx // 2, 2 * lat_dev, features), jnp.float32)],
        compiler_params=params(24),
        cost_estimate=pl.CostEstimate(
            flops=2 * ctx * keys.size * lanes, bytes_accessed=8 * keys.size, transcendentals=0
        ),
        name="probs",
    )(marks, first_pair, first_other, second_pair, second_other)
    return pl.pallas_call(
        functools.partial(
            grads_kernel, row_offsets, pair_offset, latents, first_block
        ),
        out_shape=(
            jax.ShapeDtypeStruct((lat_dev, features), jnp.bfloat16),
            jax.ShapeDtypeStruct((events_dev, features), jnp.bfloat16),
            jax.ShapeDtypeStruct((events_dev, features), jnp.bfloat16),
        ),
        in_specs=[vmem] * 7,
        out_specs=(vmem,) * 3,
        scratch_shapes=[
            pltpu.VMEM((ctx // 2, 2 * lat_dev, width), jnp.float32),
            pltpu.VMEM((ctx // 2, 2 * lat_dev, features), jnp.float32),
            pltpu.VMEM((ctx - first_block, events_dev, lanes), jnp.float32),
            pltpu.VMEM((ctx, events_dev, lanes), jnp.bfloat16),
        ],
        compiler_params=params(24),
        name="grads",
    )(probs, used_keys, used_values, proj, wide_q, row_pair, row_far)


def solution(mesh):
    in_specs = (
        P("ctx", None),
        P("ctx", None),
        P(),
        P(None, "hd"),
        P("hd", None),
        P("hd", "ctx"),
        P("ctx", "hd"),
        P("ctx", "hd"),
        P("ctx", "hd"),
        P(),
        P(),
    )
    out_specs = (P("ctx", "hd"), P("ctx", "hd"), P("ctx", "hd"))
    ctx, hd = mesh.shape["ctx"], mesh.shape["hd"]

    def per_device(*arrays):
        lat_dev, features = arrays[6].shape
        fits = ctx * arrays[7].size * arrays[7].dtype.itemsize <= 2 * 1024 * 1024
        powers = ctx == 8 and hd >= 2 and ctx & (ctx - 1) == 0 and hd & (hd - 1) == 0
        aligned = 2 * lat_dev == 8 and features % HDIM == 0 and lat_dev <= Q_ROWS
        if fits and powers and aligned:
            return per_device_packed(*arrays)
        return per_device_streamed(*arrays)

    return jax.shard_map(
        per_device, mesh=mesh, in_specs=in_specs, out_specs=out_specs, check_vma=False
    )
```
